256 devices in a mesh: row: 32 (over y_hi, z, core), rep: 8 (over x, y_lo).
Axes of the slice: x: 4, y: 4 (y_hi: 2, y_lo: 2; y = y_hi * 2 + y_lo), z: 8, core: 2. Of those that a mesh axis runs over, the one named last changes fastest.
Arguments:
- features: bfloat16 [65536, 256], P(('row', 'rep')), may hold values from -6 to 6
- tiles: bfloat16 [16384, 256, 256], P(('row', 'rep')), may hold values from -0.078125 to 0.078125
- tile_target: int32 [256, 64], P(('row', 'rep')), may hold values from 0 to 7
- tile_count: int32 [256, 32], P(('row', 'rep')), may hold values from 0 to 2, as said below
- weight: bfloat16 [256, 256], replicated, may hold values from -0.375 to 0.375
- cotangent: bfloat16 [65536, 256], P(('row', 'rep')), may hold values from -6 to 6
Outputs:
- hidden_out: bfloat16 [65536, 256], P(('row', 'rep'))
- feature_grad: bfloat16 [65536, 256], P(('row', 'rep'))
- weight_grad: float32 [256, 256], replicated
The draws below stay inside these ranges and needn't reach their ends.
Inputs may be any that keep to these rules, and one draw needn't show every extreme that they name: Slot j of source partition c is live exactly when j < tile_count; in every draw some block list has all 2 slots of every source partition live. `tile_target`: read only where the slot is live.
All inputs are finite; a program needn't handle non-finite values.
Results may differ from the reference program's by a relative error of at most 0.027.
Values may be sent and summed in bfloat16 or wider, within the bound.
A program may use at most 128 MiB of HBM per device.

```python
import jax
import jax.numpy as jnp
from jax import lax

F = 256
TILE = 256
PER_SRC = 2
BLOCKS = 256
NODES = 65536
N_ROW = 32
N_REP = 8


def draw_tile_count(key, part):
    key = jax.random.fold_in(key, 7)
    key_first, key_second, key_full, key_slots = jax.random.split(key, 4)
    lists = N_ROW * N_REP
    first = jax.random.randint(key_first, (lists, 1), 0, 9)
    second = jax.random.randint(key_second, (lists, 1), 0, 9)
    level = jnp.minimum(1 + first * second // 8, 8)
    chosen = jax.random.randint(key_full, (), 0, lists)
    level = jnp.where(jnp.arange(lists)[:, None] == chosen, 8, level)
    rolls = jax.random.randint(key_slots, (lists, N_ROW, PER_SRC), 0, 8)
    return jnp.sum((rolls < level[:, :, None]).astype(jnp.int32), axis=2).astype(jnp.int32)


def touch_ends(array, rng, smallest, high):
    longest = array.shape.index(max(array.shape))
    spots = []
    for shift in (0, 1):
        where = [jax.random.randint(jax.random.fold_in(rng, axis), (), 0, length) for axis, length in enumerate(array.shape)]
        where[longest] = (where[longest] + shift) % array.shape[longest]
        spots.append(tuple(where))
    return array.at[spots[0]].set(smallest).at[spots[1]].set(high)


def level_of(stream_key, shape, shards, low, largest):
    level, own = 1.0, jax.random.fold_in(stream_key, 6)
    for dim, blocks in shards:
        steps = jnp.exp(jax.random.uniform(jax.random.fold_in(own, dim), (blocks,), jnp.float32, low / len(shards), largest / len(shards)))
        level = level * jnp.repeat(steps, shape[dim] // blocks).reshape([-1 if axis == dim else 1 for axis in range(len(shape))])
    return level


def noise(stream_key, shape, scale, reach, cuts=(), held_as=jnp.bfloat16):
    loudness = level_of(stream_key, shape, cuts, -0.22, 0.18) if cuts else 1.0
    result = jax.random.normal(stream_key, shape, jnp.float32) * scale * loudness
    return jnp.minimum(jnp.maximum(result, -reach), reach).astype(held_as)


def setup_inputs(seed: int = 0) -> dict:
    key_of = jax.random.split(jax.random.key(seed), 7)
    return {
        "features": noise(key_of[0], (NODES, F), 1.0, 6.0, ((0, 256),)),
        "tiles": noise(key_of[1], (BLOCKS * N_ROW * PER_SRC, TILE, TILE), (TILE * N_ROW * PER_SRC * 3 // 8) ** -0.5, 0.078125, ((0, 256),)),
        "tile_target": touch_ends(jax.random.randint(key_of[2], (BLOCKS, N_ROW * PER_SRC), 0, N_REP), jax.random.fold_in(key_of[2], 1), 0, N_REP - 1).astype(jnp.int32),
        "tile_count": draw_tile_count(jax.random.fold_in(key_of[6], 71), 0),
        "weight": noise(key_of[4], (F, F), F ** -0.5, 0.375),
        "cotangent": noise(key_of[5], (NODES, F), 1.0, 6.0, ((0, 256),)),
    }


def reference(features, tiles, tile_target, tile_count, weight, cotangent):
    block_rows = features.reshape(N_ROW, N_REP, TILE, F)
    tile_grid = tiles.reshape(N_ROW, N_REP, N_ROW, PER_SRC, TILE, TILE)
    slot_index = jnp.arange(PER_SRC, dtype=jnp.int32)
    counts = tile_count.reshape(N_ROW, N_REP, N_ROW)
    live = (slot_index[None, None, None, :] < counts[..., None]).astype(jnp.float32)
    targets = tile_target.reshape(N_ROW, N_REP, N_ROW, PER_SRC)
    select = jax.nn.one_hot(targets, N_REP, dtype=jnp.float32) * live[..., None]
    source_rows = jnp.swapaxes(block_rows, 0, 1).astype(jnp.float32)

    def forward_rep(tile_set, select_set, source_set):
        products = jnp.einsum("cjtu,cuf->cjtf", tile_set.astype(jnp.float32), source_set,
                              precision=lax.Precision.HIGHEST)
        return jnp.einsum("cjq,cjtf->qtf", select_set, products, precision=lax.Precision.HIGHEST)

    def forward_row(row_inputs):
        tile_row, select_row = row_inputs
        return jnp.sum(jax.vmap(forward_rep)(tile_row, select_row, source_rows), axis=0)

    aggregate = lax.map(forward_row, (tile_grid, select)).reshape(NODES, F)
    aggregate_b = aggregate.astype(jnp.bfloat16)
    pre = jnp.dot(aggregate_b, weight, preferred_element_type=jnp.float32)
    sigma = jax.nn.sigmoid(pre)
    hidden_out = (pre * sigma).astype(jnp.bfloat16)
    grad_pre = (cotangent.astype(jnp.float32) * sigma * (1.0 + pre * (1.0 - sigma))).astype(jnp.bfloat16)
    weight_grad = jnp.dot(aggregate_b.T, grad_pre, preferred_element_type=jnp.float32)
    dagg = jnp.dot(grad_pre, weight.T, preferred_element_type=jnp.float32).astype(jnp.bfloat16)
    dagg_grid = dagg.reshape(N_ROW, N_REP, TILE, F).astype(jnp.float32)

    def backward_rep(tile_set, select_set, dagg_row):
        picked = jnp.einsum("cjq,qtf->cjtf", select_set, dagg_row, precision=lax.Precision.HIGHEST)
        term = jnp.einsum("cjtu,cjtf->cuf", tile_set.astype(jnp.float32), picked,
                          precision=lax.Precision.HIGHEST)
        return lax.optimization_barrier(term.astype(jnp.bfloat16)).astype(jnp.float32)

    def backward_row(carry, row_inputs):
        tile_row, select_row, dagg_row = row_inputs
        terms = jax.vmap(backward_rep, in_axes=(0, 0, None))(tile_row, select_row, dagg_row)
        return carry + jnp.swapaxes(terms, 0, 1), None

    start_sum = jnp.zeros((N_ROW, N_REP, TILE, F), jnp.float32)
    summed, trail = lax.scan(backward_row, start_sum, (tile_grid, select, dagg_grid))
    feature_grad = summed.reshape(NODES, F).astype(jnp.bfloat16)
    return (hidden_out, feature_grad, weight_grad)
```

```python
import jax
import jax.numpy as jnp
from jax import lax
from jax.experimental import pallas as pl
from jax.experimental.pallas import tpu as pltpu
from jax.sharding import PartitionSpec as P

MESH = pl.DeviceIdType.MESH
F32 = jnp.float32
BF16 = jnp.bfloat16
T = 256
HALF = 128
NZ = 8
NX = 4
NQ = 8
NC = 32
SLOTS = 64
TILE_PARTS = 8
SENDS = 128


def kernel(
    x_ref, tiles_ref, target_ref, count_ref, w_ref, ct_ref,
    hidden_ref, fgrad_ref, wgrad_ref,
    feat, tile, run, last_at, dt,
    b_half_out, b_half_in, b_full_out, b_full_in, b_y_out, b_y_in, b_keep,
    e_sib_out, e_sib_in, e_acc, e_far_out, e_half_in, e_out, e_in, e_y_out, e_y_in,
    w_term, w_in, w_a, w_b, w_c, w_sib_in, w_y_in, w_z_in, w_d, w_e, w_all,
    tile_sem, snd, rcv,
):
    row, rep = lax.axis_index("row"), lax.axis_index("rep")
    k, z, yh = row % 2, (row // 2) % NZ, row // (2 * NZ)
    x, yl = rep // 2, rep % 2

    def block(yh_, z_, k_):
        return yh_ * (2 * NZ) + z_ * 2 + k_

    me = row
    sib = (block(yh, z, 1 - k), rep)
    far_y = (block(1 - yh, z, k), rep)
    z_next = [(block(yh, (z + 1) % NZ, k), rep), (block(yh, (z + NZ - 1) % NZ, k), rep)]
    x_next = [(row, ((x + 1) % NX) * 2 + yl), (row, ((x + NX - 1) % NX) * 2 + yl)]
    near_y = (row, x * 2 + 1 - yl)

    def z_peer(d):
        return (block(yh, (z + d) % NZ, k), rep)

    def rep_peer(d):
        return (row, (rep + d) % NQ)

    number = {}
    started = []

    def sem_of(name):
        return number.setdefault(name, len(number))

    def post(name, src, dst, device):
        i = sem_of(name)
        copy = pltpu.make_async_remote_copy(
            src_ref=src, dst_ref=dst, send_sem=snd.at[i], recv_sem=rcv.at[i],
            device_id=device, device_id_type=MESH,
        )
        copy.start()
        started.append(copy)

    def arrive(name, dst, device):
        i = sem_of(name)
        pltpu.make_async_remote_copy(
            src_ref=dst, dst_ref=dst, send_sem=snd.at[i], recv_sem=rcv.at[i],
            device_id=device, device_id_type=MESH,
        ).wait_recv()

    loads = []
    per = SLOTS // TILE_PARTS
    for i in range(TILE_PARTS):
        copy = pltpu.make_async_copy(
            tiles_ref.at[pl.ds(i * per, per)], tile.at[pl.ds(i * per, per)], tile_sem.at[i]
        )
        copy.start()
        loads.append(copy)

    barrier = pltpu.get_barrier_semaphore()
    peers = [sib, far_y] + [z_peer(d) for d in range(1, NZ)] + [rep_peer(d) for d in range(1, NQ)]
    for peer in peers:
        pl.semaphore_signal(barrier, inc=1, device_id=peer, device_id_type=MESH)
    feat[me] = x_ref[...]
    run[SLOTS] = jnp.zeros((T, T), F32)
    dt[NQ] = jnp.zeros((T, T), BF16)
    pl.semaphore_wait(barrier, len(peers))

    rows_of = [pl.ds(0, HALF), pl.ds(HALF, HALF)]

    def yh_of(s):
        return yh if s == 0 else 1 - yh

    def z_at(way, t):
        return (z + NZ - t) % NZ if way == 0 else (z + t) % NZ

    def forward(c, p, last):
        prod = jnp.dot(
            tile[pl.ds(2 * c, 2)].reshape(2 * T, T), feat[c], preferred_element_type=F32
        )
        live = count_ref[0, c]
        for j in range(2):
            target = target_ref[0, 2 * c + j]
            before = jnp.int32(SLOTS)
            for q in range(NQ):
                before = jnp.where(target == q, last[q], before)
            run[2 * p + j] = prod[j * T : (j + 1) * T] + run[before]
            last = tuple(
                jnp.where((target == q) & (live > j), 2 * p + j, last[q]) for q in range(NQ)
            )
        return last

    def forward_group(last, start, size, t, core):
        def body(i, last):
            way, s = i % 2, i // 2
            if t == 0 or t == NZ // 2:
                way, s = 0, i
            zt = (z + jnp.where(way == 0, NZ - t, t)) % NZ
            c = block(jnp.where(s == 0, yh, 1 - yh), zt, core)
            return forward(c, start + i, last)

        return lax.fori_loop(0, size, body, last)

    post("ay", feat.at[me], feat.at[me], far_y)
    for way in range(2):
        post(("az", way, 1, 0), feat.at[me], feat.at[me], z_next[way])
    post(("as", 0, 0), feat.at[me], feat.at[me], sib)
    other = block(1 - yh, z, k)
    arrive("ay", feat.at[other], far_y)
    for way in range(2):
        post(("az", way, 1, 1), feat.at[other], feat.at[other], z_next[way])
    post(("as", 0, 1), feat.at[other], feat.at[other], sib)
    for copy in loads:
        copy.wait()
    last = (jnp.int32(SLOTS),) * NQ
    last = forward_group(last, 0, 2, 0, k)
    place = 2

    def sib_arrive(t):
        for s in range(2):
            if t == 0:
                c = block(yh_of(s), z, 1 - k)
                arrive(("as", 0, s), feat.at[c], sib)
                continue
            for way in range(2):
                c = block(yh_of(s), z_at(way, t), 1 - k)
                ref = feat.at[c, rows_of[way]] if t == NZ // 2 else feat.at[c]
                arrive(("as", t, s, way), ref, sib)

    for t in range(1, NZ // 2 + 1):
        for s in range(2):
            for way in range(2):
                c = block(yh_of(s), z_at(way, t), k)
                whole = feat.at[c]
                half = feat.at[c, rows_of[way]]
                ref = half if t == NZ // 2 else whole
                arrive(("az", way, t, s), ref, z_next[1 - way])
                if t < NZ // 2:
                    on = half if t + 1 == NZ // 2 else whole
                    post(("az", way, t + 1, s), on, on, z_next[way])
                post(("as", t, s, way), ref, ref, sib)
        size = 2 if t == NZ // 2 else 4
        last = forward_group(last, place, size, t, k)
        place += size
        sib_arrive(t - 1)
        size = 2 if t == 1 else 4
        last = forward_group(last, place, size, t - 1, 1 - k)
        place += size
    sib_arrive(NZ // 2)
    last = forward_group(last, place, 2, NZ // 2, 1 - k)
    for q in range(NQ):
        last_at[q] = last[q]

    def partial(q, rows):
        return run[last_at[q], rows]

    every = pl.ds(0, T)

    def yl_of(s):
        return 1 - yl if s == 0 else yl

    for s in range(2):
        for way in range(2):
            q = ((x + 2) % NX) * 2 + yl_of(s)
            i = 2 * s + way
            b_half_out[i] = partial(q, rows_of[way]).astype(BF16)
            post(("bh", i), b_half_out.at[i], b_half_in.at[i], x_next[way])
    for s in range(2):
        for way in range(2):
            q = ((x + (1 if way == 0 else NX - 1)) % NX) * 2 + yl
            if s == 0:
                q = q + 1 - 2 * yl
            i = 2 * s + way
            b_full_out[i, rows_of[1 - way]] = partial(q, rows_of[1 - way]).astype(BF16)
            arrive(("bh", i), b_half_in.at[i], x_next[1 - way])
            b_full_out[i, rows_of[way]] = (
                partial(q, rows_of[way]) + b_half_in[i].astype(F32)
            ).astype(BF16)
            post(("bf", i), b_full_out.at[i], b_full_in.at[i], x_next[way])
    for s in range(2):
        for way in range(2):
            arrive(("bf", 2 * s + way), b_full_in.at[2 * s + way], x_next[1 - way])
        total = (
            partial(x * 2 + yl_of(s), every)
            + b_full_in[2 * s].astype(F32)
            + b_full_in[2 * s + 1].astype(F32)
        )
        if s == 0:
            b_y_out[...] = total.astype(BF16)
            post("by", b_y_out, b_y_in, near_y)
        else:
            b_keep[...] = total
    arrive("by", b_y_in, near_y)
    agg = (b_keep[...] + b_y_in[...].astype(F32)).astype(BF16)

    pre = jnp.dot(agg, w_ref[...], preferred_element_type=F32)
    sigma = jax.nn.sigmoid(pre)
    grad_pre = (ct_ref[...].astype(F32) * sigma * (1.0 + pre * (1.0 - sigma))).astype(BF16)
    dt[rep] = lax.dot_general(
        w_ref[...], grad_pre, (((1,), (1,)), ((), ())), preferred_element_type=F32
    ).astype(BF16)

    own = dt.at[rep]
    post("dy", own, own, near_y)
    for way in range(2):
        post(("dx", way, 0), own, own, x_next[way])
    hidden_ref[...] = (pre * sigma).astype(BF16)
    near = dt.at[x * 2 + 1 - yl]
    arrive("dy", near, near_y)
    for way in range(2):
        post(("dx", way, 1), near, near, x_next[way])
    term = lax.dot_general(agg, grad_pre, (((0,), (0,)), ((), ())), preferred_element_type=F32)
    for q in range(NQ):
        for n in range(NZ):
            top, side = 32 * q + 8 * (n // 2), HALF * (n % 2)
            w_term[q, n] = term[top : top + 8, side : side + HALF]

    def dt_at(way, t, s):
        return ((x + (NX - t if way == 0 else t)) % NX) * 2 + (yl if s == 0 else 1 - yl)

    for s in range(2):
        for way in range(2):
            q = dt_at(way, 1, s)
            arrive(("dx", way, s), dt.at[q], x_next[1 - way])
            half = dt.at[q, rows_of[way]]
            post(("dh", way, s), half, half, x_next[way])
    for d in range(1, NQ):
        post(("w1", d), w_term.at[(rep + d) % NQ], w_in.at[d - 1], rep_peer(d))
    for s in range(2):
        for way in range(2):
            half = dt.at[dt_at(way, 2, s), rows_of[way]]
            arrive(("dh", way, s), half, x_next[1 - way])

    def backward(c):
        live = count_ref[0, c]
        picked = [
            dt[jnp.where(live > j, target_ref[0, 2 * c + j], NQ)] for j in range(2)
        ]
        return jnp.dot(
            jnp.concatenate(picked, axis=1), tile[pl.ds(2 * c, 2)].reshape(2 * T, T),
            preferred_element_type=F32,
        )

    base = {4: 0, 3: 2, 2: 6, 1: 10, 0: 14}
    count = {4: 2, 3: 4, 2: 4, 1: 4, 0: 2}

    def backward_group(t, core, store):
        def body(i, carry):
            way, s = i % 2, i // 2
            if t == 0 or t == NZ // 2:
                way, s = 0, i
            zt = (z + jnp.where(way == 0, t, NZ - t)) % NZ
            c = block(jnp.where(s == 0, 1 - yh, yh), zt, core)
            store(base[t] + i, backward(c))
            return carry

        lax.fori_loop(0, count[t], body, 0)

    def for_sib(t):
        def store(i, value):
            e_sib_out[i] = value.astype(BF16)

        backward_group(t, 1 - k, store)
        part = pl.ds(base[t], count[t])
        post(("es", t), e_sib_out.at[part], e_sib_in.at[part], sib)

    def for_own(t):
        def store(i, value):
            e_acc[i] = value

        backward_group(t, k, store)

    def sib_in(t):
        part = pl.ds(base[t], count[t])
        arrive(("es", t), e_sib_in.at[part], sib)

    def chip_sum(i, rows=every):
        return e_acc[i, rows] + e_sib_in[i, rows].astype(F32)

    def near_ring(t, s):
        for way in range(2):
            i = base[t] + 2 * s + way
            o = 4 * (3 - t) + 2 * s + way
            if t == 3:
                e_out[o, rows_of[1 - way]] = chip_sum(i, rows_of[1 - way]).astype(BF16)
                arrive(("eh", way, s), e_half_in.at[2 * s + way], z_next[1 - way])
                e_out[o, rows_of[way]] = (
                    chip_sum(i, rows_of[way]) + e_half_in[2 * s + way].astype(F32)
                ).astype(BF16)
            else:
                arrive(("er", o - 4), e_in.at[o - 4], z_next[1 - way])
                e_out[o] = (chip_sum(i) + e_in[o - 4].astype(F32)).astype(BF16)
            post(("er", o), e_out.at[o], e_in.at[o], z_next[way])

    for_sib(4)
    for_own(4)
    for_sib(3)
    sib_in(4)
    for s in range(2):
        e_far_out[s] = chip_sum(s).astype(BF16)
        for way in range(2):
            post(
                ("eh", way, s), e_far_out.at[s, rows_of[way]], e_half_in.at[2 * s + way],
                z_next[way],
            )
    for_own(3)
    for_sib(2)
    for d in range(1, NQ):
        arrive(("w1", d), w_in.at[d - 1], rep_peer(NQ - d))
    total = w_term[rep]
    for d in range(1, NQ):
        total = total + w_in[d - 1]
    w_a[...] = total
    post("w2", w_a, w_sib_in, sib)
    sib_in(3)
    near_ring(3, 0)
    arrive("w2", w_sib_in, sib)
    w_b[...] = w_a[...] + w_sib_in[...]
    post("w3", w_b, w_y_in, far_y)
    near_ring(3, 1)
    for_own(2)
    for_sib(1)
    arrive("w3", w_y_in, far_y)
    w_c[...] = w_b[...] + w_y_in[...]
    for d in range(1, NZ):
        post(("w4", d), w_c.at[(z + d) % NZ], w_z_in.at[d - 1], z_peer(d))
    sib_in(2)
    near_ring(2, 0)
    for d in range(1, NZ):
        arrive(("w4", d), w_z_in.at[d - 1], z_peer(NZ - d))
    total = w_c[z]
    for d in range(1, NZ):
        total = total + w_z_in[d - 1]
    w_e[z] = total
    for d in range(1, NZ):
        post(("w5", d), w_e.at[z], w_e.at[z], z_peer(d))
    near_ring(2, 1)
    for_own(1)
    for_sib(0)
    for_own(0)
    sib_in(1)
    near_ring(1, 0)
    for d in range(1, NZ):
        arrive(("w5", d), w_e.at[(z + NZ - d) % NZ], z_peer(NZ - d))
    for d in range(1, NQ):
        post(("w6", d), w_e, w_all.at[rep], rep_peer(d))
    w_all[rep] = w_e[...]
    near_ring(1, 1)
    sib_in(0)
    for s in range(2):
        for way in range(2):
            arrive(("er", 8 + 2 * s + way), e_in.at[8 + 2 * s + way], z_next[1 - way])
        total = (
            chip_sum(base[0] + s)
            + e_in[8 + 2 * s].astype(F32)
            + e_in[8 + 2 * s + 1].astype(F32)
        )
        if s == 0:
            e_y_out[...] = total.astype(BF16)
            post("ey", e_y_out, e_y_in, far_y)
        else:
            e_acc[0] = total
    for d in range(1, NQ):
        arrive(("w6", d), w_all.at[(rep + NQ - d) % NQ], rep_peer(NQ - d))
    for q in range(NQ):
        for n in range(NZ):
            top, side = 32 * q + 8 * (n // 2), HALF * (n % 2)
            wgrad_ref[top : top + 8, side : side + HALF] = w_all[q, n]
    arrive("ey", e_y_in, far_y)
    fgrad_ref[...] = (e_acc[0] + e_y_in[...].astype(F32)).T.astype(BF16)
    for copy in started:
        copy.wait_send()


def local(features, tiles, tile_target, tile_count, weight, cotangent):
    vmem = pl.BlockSpec(memory_space=pltpu.VMEM)
    smem = pl.BlockSpec(memory_space=pltpu.SMEM)
    anywhere = pl.BlockSpec(memory_space=pl.ANY)

    def buf(*shape, dtype=BF16):
        return pltpu.VMEM(shape, dtype)

    return pl.pallas_call(
        kernel,
        out_shape=(
            jax.ShapeDtypeStruct((T, T), BF16),
            jax.ShapeDtypeStruct((T, T), BF16),
            jax.ShapeDtypeStruct((T, T), F32),
        ),
        in_specs=[vmem, anywhere, smem, smem, vmem, vmem],
        out_specs=(vmem, vmem, vmem),
        scratch_shapes=[
            buf(NC, T, T),
            buf(SLOTS, T, T),
            buf(SLOTS + 1, T, T, dtype=F32),
            pltpu.SMEM((NQ,), jnp.int32),
            buf(NQ + 1, T, T),
            buf(4, HALF, T),
            buf(4, HALF, T),
            buf(4, T, T),
            buf(4, T, T),
            buf(T, T),
            buf(T, T),
            buf(T, T, dtype=F32),
            buf(16, T, T),
            buf(16, T, T),
            buf(16, T, T, dtype=F32),
            buf(2, T, T),
            buf(4, HALF, T),
            buf(12, T, T),
            buf(12, T, T),
            buf(T, T),
            buf(T, T),
            buf(NQ, NZ, 8, HALF, dtype=F32),
            buf(NQ - 1, NZ, 8, HALF, dtype=F32),
            buf(NZ, 8, HALF, dtype=F32),
            buf(NZ, 8, HALF, dtype=F32),
            buf(NZ, 8, HALF, dtype=F32),
            buf(NZ, 8, HALF, dtype=F32),
            buf(NZ, 8, HALF, dtype=F32),
            buf(NZ - 1, 8, HALF, dtype=F32),
            buf(8, HALF, dtype=F32),
            buf(NZ, 8, HALF, dtype=F32),
            buf(NQ, NZ, 8, HALF, dtype=F32),
            pltpu.SemaphoreType.DMA((TILE_PARTS,)),
            pltpu.SemaphoreType.DMA((SENDS,)),
            pltpu.SemaphoreType.DMA((SENDS,)),
        ],
        compiler_params=pltpu.CompilerParams(
            collective_id=0, has_side_effects=True, vmem_limit_bytes=56 * 1024 * 1024
        ),
        name="graph_layer",
    )(features, tiles, tile_target, tile_count, weight, cotangent)


def solution(mesh):
    return jax.shard_map(
        local,
        mesh=mesh,
        in_specs=(
            P(("row", "rep"), None),
            P(("row", "rep"), None, None),
            P(("row", "rep"), None),
            P(("row", "rep"), None),
            P(),
            P(("row", "rep"), None),
        ),
        out_specs=(P(("row", "rep"), None), P(("row", "rep"), None), P()),
        check_vma=False,
    )
```

```python
import jax
import jax.numpy as jnp
from jax import lax
from jax.experimental import pallas as pl
from jax.experimental.pallas import tpu as pltpu
from jax.sharding import PartitionSpec as P

MESH = pl.DeviceIdType.MESH
F32 = jnp.float32
BF16 = jnp.bfloat16
T = 256
HALF = 128
NZ = 8
NX = 4
NQ = 8
NC = 32
SLOTS = 64
TILE_PARTS = 8
SENDS = 192


def kernel(
    x_hbm, tiles_ref, target_hbm, count_hbm, w_hbm, ct_hbm,
    hidden_ref, fgrad_ref, wgrad_ref,
    target_ref, count_ref, w_ref, ct_ref, feat, tile, run, last_at, dt,
    ba_out, ba_in, bb_out, bb_in, bn_out, bn_in, by_out, by_in, b_keep,
    e_sib_out, e_sib_in, ea_out, ea_in, eb_out, eb_in, ef_out, ef_in, ey_out, ey_in,
    w_term, w_in, w_a, w_b, w_c, w_z_in, w_e, w_all,
    tile_sem, in_sem, snd, rcv,
):
    row, rep = lax.axis_index("row"), lax.axis_index("rep")
    k, z, yh = row % 2, (row // 2) % NZ, row // (2 * NZ)
    x, yl = rep // 2, rep % 2

    def block(yh_, z_, k_):
        return yh_ * (2 * NZ) + z_ * 2 + k_

    me = row
    sib = (block(yh, z, 1 - k), rep)
    far_y = (block(1 - yh, z, k), rep)
    group = [sib, far_y, (block(1 - yh, z, 1 - k), rep)]
    z_next = [(block(yh, (z + 1) % NZ, k), rep), (block(yh, (z + NZ - 1) % NZ, k), rep)]
    x_next = [(row, ((x + 1) % NX) * 2 + yl), (row, ((x + NX - 1) % NX) * 2 + yl)]
    near_y = (row, x * 2 + 1 - yl)

    def z_peer(d):
        return (block(yh, (z + d) % NZ, k), rep)

    def rep_peer(d):
        return (row, (rep + d) % NQ)

    number = {}
    started = []

    def sem_of(name):
        return number.setdefault(name, len(number))

    def post(name, src, dst, device):
        i = sem_of(name)
        copy = pltpu.make_async_remote_copy(
            src_ref=src, dst_ref=dst, send_sem=snd.at[i], recv_sem=rcv.at[i],
            device_id=device, device_id_type=MESH,
        )
        copy.start()
        started.append(copy)

    def arrive(name, dst, device):
        i = sem_of(name)
        pltpu.make_async_remote_copy(
            src_ref=dst, dst_ref=dst, send_sem=snd.at[i], recv_sem=rcv.at[i],
            device_id=device, device_id_type=MESH,
        ).wait_recv()

    inputs = [
        (x_hbm.at[:, pl.ds(0, HALF)], feat.at[0, me]),
        (x_hbm.at[:, pl.ds(HALF, HALF)], feat.at[1, me]),
        (target_hbm, target_ref),
        (count_hbm, count_ref),
        (w_hbm, w_ref),
        (ct_hbm, ct_ref),
    ]
    inputs = [
        pltpu.make_async_copy(src, dst, in_sem.at[i]) for i, (src, dst) in enumerate(inputs)
    ]
    for copy in inputs:
        copy.start()
    loads = []
    per = SLOTS // TILE_PARTS
    for i in range(TILE_PARTS):
        copy = pltpu.make_async_copy(
            tiles_ref.at[pl.ds(i * per, per)], tile.at[pl.ds(i * per, per)], tile_sem.at[i]
        )
        copy.start()
        loads.append(copy)

    barrier = pltpu.get_barrier_semaphore()
    peers = group + [z_peer(d) for d in range(1, NZ)] + [rep_peer(d) for d in range(1, NQ)]
    for peer in peers:
        pl.semaphore_signal(barrier, inc=1, device_id=peer, device_id_type=MESH)
    run[SLOTS] = jnp.zeros((T, T), F32)
    dt[NQ] = jnp.zeros((T, T), BF16)
    pl.semaphore_wait(barrier, len(peers))

    rows_of = [pl.ds(0, HALF), pl.ds(HALF, HALF)]
    FAR = NZ // 2

    def yh_of(s):
        return yh if s == 0 else 1 - yh

    def z_at(way, t):
        return (z + NZ - t) % NZ if way == 0 else (z + t) % NZ

    def tags(h, t, s):
        if t == 0:
            return [0]
        if t == FAR and h == 0:
            return [s]
        return [0, 1]

    def piece(h, t, s, tag, core, split):
        c = block(yh_of(s), z_at(tag, t), core)
        if split:
            return feat.at[h, c, rows_of[tag]]
        return feat.at[h, c]

    def forward(c, p, last):
        prod = jnp.dot(
            tile[pl.ds(2 * c, 2)].reshape(2 * T, T),
            jnp.concatenate([feat[0, c], feat[1, c]], axis=1),
            preferred_element_type=F32,
        )
        live = count_ref[0, c]
        for j in range(2):
            target = target_ref[0, 2 * c + j]
            before = jnp.int32(SLOTS)
            for q in range(NQ):
                before = jnp.where(target == q, last[q], before)
            run[2 * p + j] = prod[j * T : (j + 1) * T] + run[before]
            last = tuple(
                jnp.where((target == q) & (live > j), 2 * p + j, last[q]) for q in range(NQ)
            )
        return last

    state = {"last": (jnp.int32(SLOTS),) * NQ, "place": 0}

    def compute(t, s, core):
        start = state["place"]
        size = 1 if t in (0, FAR) else 2

        def body(i, last):
            zt = (z + jnp.where(i == 0, NZ - t, t)) % NZ
            return forward(block(yh_of(s), zt, core), start + i, last)

        state["last"] = lax.fori_loop(0, size, body, state["last"])
        state["place"] = start + size

    def split_at(h, t):
        return h == 1 and t == FAR

    def z_post(h, s, t, tag):
        ref = piece(h, t - 1, s, tag, k, split_at(h, t))
        post(("az", h, s, t, tag), ref, ref, z_next[tag])

    def sib_post(h, t, s, tag):
        ref = piece(h, t, s, tag, k, split_at(h, t))
        post(("as", h, t, s, tag), ref, ref, sib)

    def far_post(t, tag):
        ref = piece(1, t, 0, tag, k, split_at(1, t))
        post(("af", t, tag), ref, ref, far_y)

    def sib_wait(t, s):
        for h in range(2):
            for tag in tags(h, t, s):
                arrive(
                    ("as", h, t, s, tag), piece(h, t, s, tag, 1 - k, split_at(h, t)), sib
                )

    for copy in inputs[:2]:
        copy.wait()
    own = feat.at[0, me]
    post("ay", own, own, far_y)
    for h in range(2):
        for way in range(2):
            z_post(h, 0, 1, way)
    far_post(0, 0)
    for h in range(2):
        sib_post(h, 0, 0, 0)
    arrive("ay", piece(0, 0, 1, 0, k, False), far_y)
    for way in range(2):
        z_post(0, 1, 1, way)
    sib_post(0, 0, 1, 0)
    for copy in inputs[2:4] + loads:
        copy.wait()
    compute(0, 0, k)
    def z_step(h, s, t):
        for tag in tags(h, t, s):
            ref = piece(h, t, s, tag, k, split_at(h, t))
            arrive(("az", h, s, t, tag), ref, z_next[1 - tag])
            if t < FAR and tag in tags(h, t + 1, s):
                z_post(h, s, t + 1, tag)
            if h == 1:
                far_post(t, tag)
            sib_post(h, t, s, tag)

    for t in range(1, FAR + 3):
        if t <= FAR:
            z_step(1, 0, t)
            z_step(0, 0, t)
        if t >= 2:
            sib_wait(t - 2, 1)
            compute(t - 2, 1, 1 - k)
        if t - 1 <= FAR:
            sib_wait(t - 1, 0)
            compute(t - 1, 0, 1 - k)
        if t <= FAR:
            z_step(0, 1, t)
        if t - 1 <= FAR:
            for tag in tags(1, t - 1, 1):
                arrive(("af", t - 1, tag), piece(1, t - 1, 1, tag, k, split_at(1, t - 1)), far_y)
                sib_post(1, t - 1, 1, tag)
        if t <= FAR:
            compute(t, 0, k)
        if t - 1 <= FAR:
            compute(t - 1, 1, k)
    for q in range(NQ):
        last_at[q] = state["last"][q]

    every = pl.ds(0, T)

    def partial(q, h):
        return run[last_at[q], :, h * HALF : (h + 1) * HALF]

    def q_at(way, t, s):
        return ((x + (t if way == 0 else NX - t)) % NX) * 2 + (1 - yl if s == 0 else yl)

    def near_post(i, q):
        bn_out[i] = partial(q, 1).astype(BF16)
        post(("bn", i), bn_out.at[i], bn_in.at[i], near_y)

    def a_post(i, value, way):
        ba_out[i] = value.astype(BF16)
        post(("ba", i), ba_out.at[i], ba_in.at[i], x_next[way])

    near_post(0, q_at(0, 2, 0))
    for s in range(2):
        a_post(s, partial(q_at(0, 2, s), 0), s)
    for way in range(2):
        near_post(1 + way, q_at(way, 1, 0))
    for s in range(2):
        way = 1 - s
        a_post(2 + 2 * s + way, partial(q_at(way, 1, s), 0), way)
    near_post(3, q_at(0, 0, 0))
    for s in range(2):
        arrive(("ba", s), ba_in.at[s], x_next[1 - s])
        a_post(2 + 3 * s, partial(q_at(s, 1, s), 0) + ba_in[s].astype(F32), s)
    arrive(("bn", 0), bn_in.at[0], near_y)
    bb_out[0] = (partial(q_at(0, 2, 1), 1) + bn_in[0].astype(F32)).astype(BF16)
    for way in range(2):
        post(
            ("bh", way), bb_out.at[0, rows_of[way]], bb_in.at[0, rows_of[way]], x_next[way]
        )
    for way in range(2):
        arrive(("bn", 1 + way), bn_in.at[1 + way], near_y)
        arrive(("bh", way), bb_in.at[0, rows_of[way]], x_next[1 - way])
        value = partial(q_at(way, 1, 1), 1) + bn_in[1 + way].astype(F32)
        extra = bb_in[0, rows_of[way]].astype(F32)
        keep, more = slice((1 - way) * HALF, (2 - way) * HALF), slice(way * HALF, (1 + way) * HALF)
        bb_out[1 + way, rows_of[1 - way]] = value[keep].astype(BF16)
        bb_out[1 + way, rows_of[way]] = (value[more] + extra).astype(BF16)
        post(("bb", way), bb_out.at[1 + way], bb_in.at[1 + way], x_next[way])
    for s in range(2):
        for way in range(2):
            i = 2 + 2 * s + way
            arrive(("ba", i), ba_in.at[i], x_next[1 - way])
        total = (
            partial(q_at(0, 0, s), 0)
            + ba_in[2 + 2 * s].astype(F32) + ba_in[3 + 2 * s].astype(F32)
        )
        if s == 0:
            by_out[...] = total.astype(BF16)
            post("by", by_out, by_in, near_y)
        else:
            b_keep[:, :HALF] = total
    arrive(("bn", 3), bn_in.at[3], near_y)
    for way in range(2):
        arrive(("bb", way), bb_in.at[1 + way], x_next[1 - way])
    b_keep[:, HALF:] = (
        partial(q_at(0, 0, 1), 1) + bn_in[3].astype(F32)
        + bb_in[1].astype(F32) + bb_in[2].astype(F32)
    )
    arrive("by", by_in, near_y)
    b_keep[:, :HALF] = b_keep[:, :HALF] + by_in[...].astype(F32)
    agg = b_keep[...].astype(BF16)

    for copy in inputs[4:]:
        copy.wait()
    pre = jnp.dot(agg, w_ref[...], preferred_element_type=F32)
    sigma = jax.nn.sigmoid(pre)
    grad_pre = (ct_ref[...].astype(F32) * sigma * (1.0 + pre * (1.0 - sigma))).astype(BF16)
    dt[rep] = lax.dot_general(
        w_ref[...], grad_pre, (((1,), (1,)), ((), ())), preferred_element_type=F32
    ).astype(BF16)

    sub_of = [pl.ds(HALF, HALF // 2), pl.ds(HALF + HALF // 2, HALF // 2)]

    def dt_at(way, t, s):
        return ((x + (NX - t if way == 0 else t)) % NX) * 2 + (yl if s == 0 else 1 - yl)

    def hop(name, ref, device):
        post(name, ref, ref, device)

    top, low = dt.at[rep, rows_of[0]], dt.at[rep, rows_of[1]]
    hop("dy", top, near_y)
    for way in range(2):
        hop(("da", 1, 0, way), top, x_next[way])
        hop(("db", 1, way), low, x_next[way])
    hop(("dn", 0), low, near_y)
    hidden_ref[...] = (pre * sigma).astype(BF16)
    near = dt.at[dt_at(0, 0, 1), rows_of[0]]
    arrive("dy", near, near_y)
    for way in range(2):
        hop(("da", 1, 1, way), near, x_next[way])
    term = lax.dot_general(agg, grad_pre, (((0,), (0,)), ((), ())), preferred_element_type=F32)
    for q in range(NQ):
        for n in range(NZ):
            up, side = 32 * q + 8 * (n // 2), HALF * (n % 2)
            w_term[q, n] = term[up : up + 8, side : side + HALF]

    for way in range(2):
        ref = dt.at[dt_at(way, 1, 0), rows_of[0]]
        arrive(("da", 1, 0, way), ref, x_next[1 - way])
        if way == 0:
            hop(("da", 2, 0), ref, x_next[way])
        q = dt_at(way, 1, 0)
        arrive(("db", 1, way), dt.at[q, rows_of[1]], x_next[1 - way])
        hop(("db", 2, way), dt.at[q, sub_of[way]], x_next[way])
        hop(("dn", 1 + way), dt.at[q, rows_of[1]], near_y)
    for way in (1, 0):
        ref = dt.at[dt_at(way, 1, 1), rows_of[0]]
        arrive(("da", 1, 1, way), ref, x_next[1 - way])
        if way == 1:
            hop(("da", 2, 1), ref, x_next[way])
    for way in range(2):
        ref = dt.at[dt_at(way, 2, 0), sub_of[way]]
        arrive(("db", 2, way), ref, x_next[1 - way])
        hop(("dn", 3 + way), ref, near_y)
    for d in range(1, NQ):
        post(("w1", d), w_term.at[(rep + d) % NQ], w_in.at[d - 1], rep_peer(d))
    for s in range(2):
        arrive(("da", 2, s), dt.at[dt_at(s, 2, s), rows_of[0]], x_next[1 - s])
    arrive(("dn", 0), dt.at[dt_at(0, 0, 1), rows_of[1]], near_y)
    for way in range(2):
        arrive(("dn", 1 + way), dt.at[dt_at(way, 1, 1), rows_of[1]], near_y)
    for way in range(2):
        arrive(("dn", 3 + way), dt.at[dt_at(way, 2, 1), sub_of[way]], near_y)

    def backward(c):
        live = count_ref[0, c]
        picked = [
            dt[jnp.where(live > j, target_ref[0, 2 * c + j], NQ)] for j in range(2)
        ]
        return jnp.dot(
            jnp.concatenate(picked, axis=1), tile[pl.ds(2 * c, 2)].reshape(2 * T, T),
            preferred_element_type=F32,
        )

    base = {4: 0, 3: 2, 2: 6, 1: 10, 0: 14}
    count = {4: 2, 3: 4, 2: 4, 1: 4, 0: 2}

    def backward_group(t, core, store):
        def body(i, carry):
            way, s = i % 2, i // 2
            if t == 0 or t == NZ // 2:
                way, s = 0, i
            zt = (z + jnp.where(way == 0, t, NZ - t)) % NZ
            c = block(jnp.where(s == 0, 1 - yh, yh), zt, core)
            store(base[t] + i, backward(c))
            return carry

        lax.fori_loop(0, count[t], body, 0)

    def for_sib(t):
        def store(i, value):
            e_sib_out[i] = value.astype(BF16)

        backward_group(t, 1 - k, store)
        part = pl.ds(base[t], count[t])
        post(("es", t), e_sib_out.at[part], e_sib_in.at[part], sib)

    def for_own(t):
        def store(i, value):
            run[i] = value

        backward_group(t, k, store)

    def sib_in(t):
        part = pl.ds(base[t], count[t])
        arrive(("es", t), e_sib_in.at[part], sib)

    def chip_sum(i, h):
        rows = rows_of[h]
        return run[i, rows] + e_sib_in[i, rows].astype(F32)

    quarter = HALF // 2

    def far_sum_post(t):
        for way in range(1 if t in (0, FAR) else 2):
            o = 0 if t == FAR else 7 if t == 0 else 1 + 2 * (3 - t) + way
            ef_out[o] = chip_sum(base[t] + way, 1).astype(BF16)
            post(("ef", o), ef_out.at[o], ef_in.at[o], far_y)

    def low_sum(t, way):
        o = 0 if t == FAR else 7 if t == 0 else 1 + 2 * (3 - t) + way
        arrive(("ef", o), ef_in.at[o], far_y)
        i = base[t] + (1 if t in (0, FAR) else 2 + way)
        return chip_sum(i, 1) + ef_in[o].astype(F32)

    def ring_top(t, s):
        if t == FAR:
            ea_out[s] = chip_sum(base[t] + s, 0).astype(BF16)
            post(("ea", s), ea_out.at[s], ea_in.at[s], z_next[s])
            return
        for way in (1 - s, s):
            value = chip_sum(base[t] + 2 * s + way, 0)
            o = 2 + 4 * (3 - t) + 2 * s + way
            before = o - 4 if t < 3 else s if way == s else None
            if before is not None:
                arrive(("ea", before), ea_in.at[before], z_next[1 - way])
                value = value + ea_in[before].astype(F32)
            ea_out[o] = value.astype(BF16)
            post(("ea", o), ea_out.at[o], ea_in.at[o], z_next[way])

    def ring_low(t):
        if t == FAR:
            eb_out[0] = low_sum(t, 0).astype(BF16)
            for way in range(2):
                part = pl.ds(way * quarter, quarter)
                post(("eh", way), eb_out.at[0, part], eb_in.at[0, part], z_next[way])
            return
        for way in range(2):
            value = low_sum(t, way)
            o = 1 + 2 * (3 - t) + way
            if t == 3:
                part = pl.ds(way * quarter, quarter)
                arrive(("eh", way), eb_in.at[0, part], z_next[1 - way])
                more = value[way * quarter : (way + 1) * quarter] + eb_in[0, part].astype(F32)
                keep = value[(1 - way) * quarter : (2 - way) * quarter]
                eb_out[o, part] = more.astype(BF16)
                eb_out[o, pl.ds((1 - way) * quarter, quarter)] = keep.astype(BF16)
            else:
                arrive(("eb", o - 2), eb_in.at[o - 2], z_next[1 - way])
                eb_out[o] = (value + eb_in[o - 2].astype(F32)).astype(BF16)
            post(("eb", o), eb_out.at[o], eb_in.at[o], z_next[way])

    for_sib(4)
    for_own(4)
    for_sib(3)
    sib_in(4)
    far_sum_post(4)
    ring_top(4, 0)
    ring_top(4, 1)
    for_own(3)
    sib_in(3)
    far_sum_post(3)
    ring_top(3, 0)
    ring_top(3, 1)
    for_sib(2)
    for d in range(1, NQ):
        arrive(("w1", d), w_in.at[d - 1], rep_peer(NQ - d))
    total = w_term[rep]
    for d in range(1, NQ):
        total = total + w_in[d - 1]
    w_a[...] = total
    for i in range(3):
        post(("w2", i), w_a, w_b.at[i], group[i])
    ring_low(4)
    for_own(2)
    sib_in(2)
    far_sum_post(2)
    ring_top(2, 0)
    ring_top(2, 1)
    for_sib(1)
    for i in range(3):
        arrive(("w2", i), w_b.at[i], group[i])
    w_c[...] = (w_a[...] + w_b[0]) + (w_b[1] + w_b[2])
    for d in range(1, NZ):
        post(("w4", d), w_c.at[(z + d) % NZ], w_z_in.at[d - 1], z_peer(d))
    ring_low(3)
    for_own(1)
    sib_in(1)
    far_sum_post(1)
    ring_top(1, 0)
    for_sib(0)
    for d in range(1, NZ):
        arrive(("w4", d), w_z_in.at[d - 1], z_peer(NZ - d))
    total = w_c[z]
    for d in range(1, NZ):
        total = total + w_z_in[d - 1]
    w_e[z] = total
    for d in range(1, NZ):
        post(("w5", d), w_e.at[z], w_e.at[z], z_peer(d))
    ring_top(1, 1)
    for_own(0)
    sib_in(0)
    far_sum_post(0)
    ring_low(2)
    for d in range(1, NZ):
        arrive(("w5", d), w_e.at[(z + NZ - d) % NZ], z_peer(NZ - d))
    for d in range(1, NQ):
        post(("w6", d), w_e, w_all.at[rep], rep_peer(d))
    w_all[rep] = w_e[...]
    ring_low(1)
    for s in range(2):
        i = 10 + 2 * s
        for way in range(2):
            arrive(("ea", i + way), ea_in.at[i + way], z_next[1 - way])
        total = (
            chip_sum(base[0] + s, 0) + ea_in[i].astype(F32) + ea_in[i + 1].astype(F32)
        )
        if s == 0:
            ey_out[...] = total.astype(BF16)
            post("ey", ey_out, ey_in, far_y)
        else:
            run[0, rows_of[0]] = total
    low_total = low_sum(0, 0)
    for way in range(2):
        arrive(("eb", 5 + way), eb_in.at[5 + way], z_next[1 - way])
    low_total = low_total + eb_in[5].astype(F32) + eb_in[6].astype(F32)
    fgrad_ref[:, HALF:] = low_total.T.astype(BF16)
    for d in range(1, NQ):
        arrive(("w6", d), w_all.at[(rep + NQ - d) % NQ], rep_peer(NQ - d))
    for q in range(NQ):
        for n in range(NZ):
            up, side = 32 * q + 8 * (n // 2), HALF * (n % 2)
            wgrad_ref[up : up + 8, side : side + HALF] = w_all[q, n]
    arrive("ey", ey_in, far_y)
    fgrad_ref[:, :HALF] = (run[0, rows_of[0]] + ey_in[...].astype(F32)).T.astype(BF16)
    for copy in started:
        copy.wait_send()


def local(features, tiles, tile_target, tile_count, weight, cotangent):
    vmem = pl.BlockSpec(memory_space=pltpu.VMEM)
    hbm = pl.BlockSpec(memory_space=pltpu.HBM)

    def buf(*shape, dtype=BF16):
        return pltpu.VMEM(shape, dtype)

    return pl.pallas_call(
        kernel,
        out_shape=(
            jax.ShapeDtypeStruct((T, T), BF16),
            jax.ShapeDtypeStruct((T, T), BF16),
            jax.ShapeDtypeStruct((T, T), F32),
        ),
        in_specs=[hbm] * 6,
        out_specs=(vmem, vmem, vmem),
        scratch_shapes=[
            pltpu.SMEM((1, SLOTS), jnp.int32),
            pltpu.SMEM((1, NC), jnp.int32),
            buf(T, T),
            buf(T, T),
            buf(2, NC, T, HALF),
            buf(SLOTS, T, T),
            buf(SLOTS + 1, T, T, dtype=F32),
            pltpu.SMEM((NQ,), jnp.int32),
            buf(NQ + 1, T, T),
            buf(6, T, HALF),
            buf(6, T, HALF),
            buf(3, T, HALF),
            buf(3, T, HALF),
            buf(4, T, HALF),
            buf(4, T, HALF),
            buf(T, HALF),
            buf(T, HALF),
            buf(T, T, dtype=F32),
            buf(16, T, T),
            buf(16, T, T),
            buf(14, HALF, T),
            buf(14, HALF, T),
            buf(7, HALF, T),
            buf(7, HALF, T),
            buf(8, HALF, T),
            buf(8, HALF, T),
            buf(HALF, T),
            buf(HALF, T),
            buf(NQ, NZ, 8, HALF, dtype=F32),
            buf(NQ - 1, NZ, 8, HALF, dtype=F32),
            buf(NZ, 8, HALF, dtype=F32),
            buf(3, NZ, 8, HALF, dtype=F32),
            buf(NZ, 8, HALF, dtype=F32),
            buf(NZ - 1, 8, HALF, dtype=F32),
            buf(NZ, 8, HALF, dtype=F32),
            buf(NQ, NZ, 8, HALF, dtype=F32),
            pltpu.SemaphoreType.DMA((TILE_PARTS,)),
            pltpu.SemaphoreType.DMA((6,)),
            pltpu.SemaphoreType.DMA((SENDS,)),
            pltpu.SemaphoreType.DMA((SENDS,)),
        ],
        compiler_params=pltpu.CompilerParams(
            collective_id=0, has_side_effects=True, vmem_limit_bytes=46 * 1024 * 1024
        ),
        name="graph_layer",
    )(*[
        pltpu.with_memory_space_constraint(value, pltpu.HBM)
        for value in (features, tiles, tile_target, tile_count, weight, cotangent)
    ])


def solution(mesh):
    return jax.shard_map(
        local,
        mesh=mesh,
        in_specs=(
            P(("row", "rep"), None),
            P(("row", "rep"), None, None),
            P(("row", "rep"), None),
            P(("row", "rep"), None),
            P(),
            P(("row", "rep"), None),
        ),
        out_specs=(P(("row", "rep"), None), P(("row", "rep"), None), P()),
        check_vma=False,
    )
```

```python
import jax
import jax.numpy as jnp
from jax import lax
from jax.experimental import pallas as pl
from jax.experimental.pallas import tpu as pltpu
from jax.sharding import PartitionSpec as P

MESH = pl.DeviceIdType.MESH
F32 = jnp.float32
BF16 = jnp.bfloat16
T = 256
HALF = 128
NZ = 8
NX = 4
NQ = 8
NC = 32
SLOTS = 64
TILE_PARTS = 8
SENDS = 192


def kernel(
    x_hbm, tiles_ref, target_hbm, count_hbm, w_hbm, ct_hbm,
    hidden_ref, fgrad_ref, wgrad_ref,
    target_ref, count_ref, w_ref, ct_ref, feat, tile, run, last_at, dt,
    ba_out, ba_in, bb_out, bb_in, bn_out, bn_in, by_out, by_in, b_keep,
    e_sib_out, e_sib_in, ea_out, ea_in, eb_out, eb_in, ef_out, ef_in, ey_out, ey_in,
    w_term, w_in, w_a, w_b, w_c, w_z_in, w_e, w_all,
    tile_sem, in_sem, snd, rcv,
):
    row, rep = lax.axis_index("row"), lax.axis_index("rep")
    k, z, yh = row % 2, (row // 2) % NZ, row // (2 * NZ)
    x, yl = rep // 2, rep % 2

    def block(yh_, z_, k_):
        return yh_ * (2 * NZ) + z_ * 2 + k_

    me = row
    sib = (block(yh, z, 1 - k), rep)
    far_y = (block(1 - yh, z, k), rep)
    group = [sib, far_y, (block(1 - yh, z, 1 - k), rep)]
    z_next = [(block(yh, (z + 1) % NZ, k), rep), (block(yh, (z + NZ - 1) % NZ, k), rep)]
    x_next = [(row, ((x + 1) % NX) * 2 + yl), (row, ((x + NX - 1) % NX) * 2 + yl)]
    near_y = (row, x * 2 + 1 - yl)

    def z_peer(d):
        return (block(yh, (z + d) % NZ, k), rep)

    def rep_peer(d):
        return (row, (rep + d) % NQ)

    number = {}
    started = []

    def sem_of(name):
        return number.setdefault(name, len(number))

    def post(name, src, dst, device):
        i = sem_of(name)
        copy = pltpu.make_async_remote_copy(
            src_ref=src, dst_ref=dst, send_sem=snd.at[i], recv_sem=rcv.at[i],
            device_id=device, device_id_type=MESH,
        )
        copy.start()
        started.append(copy)

    def arrive(name, dst, device):
        i = sem_of(name)
        pltpu.make_async_remote_copy(
            src_ref=dst, dst_ref=dst, send_sem=snd.at[i], recv_sem=rcv.at[i],
            device_id=device, device_id_type=MESH,
        ).wait_recv()

    inputs = [
        (x_hbm.at[:, pl.ds(0, HALF)], feat.at[0, me]),
        (x_hbm.at[:, pl.ds(HALF, HALF)], feat.at[1, me]),
        (target_hbm, target_ref),
        (count_hbm, count_ref),
        (w_hbm, w_ref),
        (ct_hbm, ct_ref),
    ]
    inputs = [
        pltpu.make_async_copy(src, dst, in_sem.at[i]) for i, (src, dst) in enumerate(inputs)
    ]
    for copy in inputs:
        copy.start()
    loads = []
    per = SLOTS // TILE_PARTS
    for i in range(TILE_PARTS):
        copy = pltpu.make_async_copy(
            tiles_ref.at[pl.ds(i * per, per)], tile.at[pl.ds(i * per, per)], tile_sem.at[i]
        )
        copy.start()
        loads.append(copy)

    barrier = pltpu.get_barrier_semaphore()
    peers = group + [z_peer(d) for d in range(1, NZ)] + [rep_peer(d) for d in range(1, NQ)]
    for peer in peers:
        pl.semaphore_signal(barrier, inc=1, device_id=peer, device_id_type=MESH)
    run[SLOTS] = jnp.zeros((T, T), F32)
    dt[NQ] = jnp.zeros((T, T), BF16)
    pl.semaphore_wait(barrier, len(peers))

    rows_of = [pl.ds(0, HALF), pl.ds(HALF, HALF)]
    FAR = NZ // 2

    def yh_of(s):
        return yh if s == 0 else 1 - yh

    def z_at(way, t):
        return (z + NZ - t) % NZ if way == 0 else (z + t) % NZ

    def tags(h, t, s):
        if t == 0:
            return [0]
        if t == FAR and h == 0:
            return [s]
        return [0, 1]

    def piece(h, t, s, tag, core, split):
        c = block(yh_of(s), z_at(tag, t), core)
        if split:
            return feat.at[h, c, rows_of[tag]]
        return feat.at[h, c]

    def forward(c, p, last):
        prod = jnp.dot(
            tile[pl.ds(2 * c, 2)].reshape(2 * T, T),
            jnp.concatenate([feat[0, c], feat[1, c]], axis=1),
            preferred_element_type=F32,
        )
        live = count_ref[0, c]
        for j in range(2):
            target = target_ref[0, 2 * c + j]
            before = jnp.int32(SLOTS)
            for q in range(NQ):
                before = jnp.where(target == q, last[q], before)
            run[2 * p + j] = prod[j * T : (j + 1) * T] + run[before]
            last = tuple(
                jnp.where((target == q) & (live > j), 2 * p + j, last[q]) for q in range(NQ)
            )
        return last

    state = {"last": (jnp.int32(SLOTS),) * NQ, "place": 0}

    def compute(t, s, core):
        start = state["place"]
        size = 1 if t in (0, FAR) else 2

        def body(i, last):
            zt = (z + jnp.where(i == 0, NZ - t, t)) % NZ
            return forward(block(yh_of(s), zt, core), start + i, last)

        state["last"] = lax.fori_loop(0, size, body, state["last"])
        state["place"] = start + size

    def split_at(h, t):
        return h == 1 and t == FAR

    def z_post(h, s, t, tag):
        ref = piece(h, t - 1, s, tag, k, split_at(h, t))
        post(("az", h, s, t, tag), ref, ref, z_next[tag])

    def sib_post(h, t, s, tag):
        ref = piece(h, t, s, tag, k, split_at(h, t))
        post(("as", h, t, s, tag), ref, ref, sib)

    def far_post(t, tag):
        ref = piece(1, t, 0, tag, k, split_at(1, t))
        post(("af", t, tag), ref, ref, far_y)

    def sib_wait(t, s):
        for h in range(2):
            for tag in tags(h, t, s):
                arrive(
                    ("as", h, t, s, tag), piece(h, t, s, tag, 1 - k, split_at(h, t)), sib
                )

    for copy in inputs[:2]:
        copy.wait()
    own = feat.at[0, me]
    post("ay", own, own, far_y)
    for h in range(2):
        for way in range(2):
            z_post(h, 0, 1, way)
    far_post(0, 0)
    for h in range(2):
        sib_post(h, 0, 0, 0)
    arrive("ay", piece(0, 0, 1, 0, k, False), far_y)
    for way in range(2):
        z_post(0, 1, 1, way)
    sib_post(0, 0, 1, 0)
    for copy in inputs[2:4] + loads:
        copy.wait()
    compute(0, 0, k)
    def z_step(h, s, t):
        for tag in tags(h, t, s):
            ref = piece(h, t, s, tag, k, split_at(h, t))
            arrive(("az", h, s, t, tag), ref, z_next[1 - tag])
            if t < FAR and tag in tags(h, t + 1, s):
                z_post(h, s, t + 1, tag)
            if h == 1:
                far_post(t, tag)
            sib_post(h, t, s, tag)

    for t in range(1, FAR + 3):
        if t <= FAR:
            z_step(1, 0, t)
            z_step(0, 0, t)
        if t >= 2:
            sib_wait(t - 2, 1)
            compute(t - 2, 1, 1 - k)
        if t - 1 <= FAR:
            sib_wait(t - 1, 0)
            compute(t - 1, 0, 1 - k)
        if t <= FAR:
            z_step(0, 1, t)
        if t - 1 <= FAR:
            for tag in tags(1, t - 1, 1):
                arrive(("af", t - 1, tag), piece(1, t - 1, 1, tag, k, split_at(1, t - 1)), far_y)
                sib_post(1, t - 1, 1, tag)
        if t <= FAR:
            compute(t, 0, k)
        if t - 1 <= FAR:
            compute(t - 1, 1, k)
    for q in range(NQ):
        last_at[q] = state["last"][q]

    every = pl.ds(0, T)

    def partial(q, h):
        return run[last_at[q], :, h * HALF : (h + 1) * HALF]

    def q_at(way, t, s):
        return ((x + (t if way == 0 else NX - t)) % NX) * 2 + (1 - yl if s == 0 else yl)

    def near_post(i, q):
        bn_out[i] = partial(q, 1).astype(BF16)
        post(("bn", i), bn_out.at[i], bn_in.at[i], near_y)

    def a_post(i, value, way):
        ba_out[i] = value.astype(BF16)
        post(("ba", i), ba_out.at[i], ba_in.at[i], x_next[way])

    near_post(0, q_at(0, 2, 0))
    for s in range(2):
        a_post(s, partial(q_at(0, 2, s), 0), s)
    for way in range(2):
        near_post(1 + way, q_at(way, 1, 0))
    for s in range(2):
        way = 1 - s
        a_post(2 + 2 * s + way, partial(q_at(way, 1, s), 0), way)
    near_post(3, q_at(0, 0, 0))
    for s in range(2):
        arrive(("ba", s), ba_in.at[s], x_next[1 - s])
        a_post(2 + 3 * s, partial(q_at(s, 1, s), 0) + ba_in[s].astype(F32), s)
    arrive(("bn", 0), bn_in.at[0], near_y)
    bb_out[0] = (partial(q_at(0, 2, 1), 1) + bn_in[0].astype(F32)).astype(BF16)
    for way in range(2):
        post(
            ("bh", way), bb_out.at[0, rows_of[way]], bb_in.at[0, rows_of[way]], x_next[way]
        )
    for way in range(2):
        arrive(("bn", 1 + way), bn_in.at[1 + way], near_y)
        arrive(("bh", way), bb_in.at[0, rows_of[way]], x_next[1 - way])
        value = partial(q_at(way, 1, 1), 1) + bn_in[1 + way].astype(F32)
        extra = bb_in[0, rows_of[way]].astype(F32)
        keep, more = slice((1 - way) * HALF, (2 - way) * HALF), slice(way * HALF, (1 + way) * HALF)
        bb_out[1 + way, rows_of[1 - way]] = value[keep].astype(BF16)
        bb_out[1 + way, rows_of[way]] = (value[more] + extra).astype(BF16)
        post(("bb", way), bb_out.at[1 + way], bb_in.at[1 + way], x_next[way])
    for s in range(2):
        for way in range(2):
            i = 2 + 2 * s + way
            arrive(("ba", i), ba_in.at[i], x_next[1 - way])
        total = (
            partial(q_at(0, 0, s), 0)
            + ba_in[2 + 2 * s].astype(F32) + ba_in[3 + 2 * s].astype(F32)
        )
        if s == 0:
            by_out[...] = total.astype(BF16)
            post("by", by_out, by_in, near_y)
        else:
            b_keep[:, :HALF] = total
    arrive(("bn", 3), bn_in.at[3], near_y)
    for way in range(2):
        arrive(("bb", way), bb_in.at[1 + way], x_next[1 - way])
    b_keep[:, HALF:] = (
        partial(q_at(0, 0, 1), 1) + bn_in[3].astype(F32)
        + bb_in[1].astype(F32) + bb_in[2].astype(F32)
    )
    arrive("by", by_in, near_y)
    b_keep[:, :HALF] = b_keep[:, :HALF] + by_in[...].astype(F32)
    agg = b_keep[...].astype(BF16)

    for copy in inputs[4:]:
        copy.wait()
    pre = jnp.dot(agg, w_ref[...], preferred_element_type=F32)
    sigma = jax.nn.sigmoid(pre)
    grad_pre = (ct_ref[...].astype(F32) * sigma * (1.0 + pre * (1.0 - sigma))).astype(BF16)
    dt[rep] = lax.dot_general(
        w_ref[...], grad_pre, (((1,), (1,)), ((), ())), preferred_element_type=F32
    ).astype(BF16)

    sub_of = [pl.ds(HALF, HALF // 2), pl.ds(HALF + HALF // 2, HALF // 2)]

    def dt_at(way, t, s):
        return ((x + (NX - t if way == 0 else t)) % NX) * 2 + (yl if s == 0 else 1 - yl)

    def hop(name, ref, device):
        post(name, ref, ref, device)

    top, low = dt.at[rep, rows_of[0]], dt.at[rep, rows_of[1]]
    hop("dy", top, near_y)
    for way in range(2):
        hop(("da", 1, 0, way), top, x_next[way])
        hop(("db", 1, way), low, x_next[way])
    hop(("dn", 0), low, near_y)
    hidden_ref[...] = (pre * sigma).astype(BF16)
    near = dt.at[dt_at(0, 0, 1), rows_of[0]]
    arrive("dy", near, near_y)
    for way in range(2):
        hop(("da", 1, 1, way), near, x_next[way])
    term = lax.dot_general(agg, grad_pre, (((0,), (0,)), ((), ())), preferred_element_type=F32)
    for q in range(NQ):
        pieces = []
        for n in range(NZ):
            up, side = 32 * q + 8 * (n // 2), HALF * (n % 2)
            pieces.append(term[up : up + 8, side : side + HALF])
        w_term[q] = jnp.concatenate(pieces, axis=0).astype(BF16)

    for way in range(2):
        ref = dt.at[dt_at(way, 1, 0), rows_of[0]]
        arrive(("da", 1, 0, way), ref, x_next[1 - way])
        if way == 0:
            hop(("da", 2, 0), ref, x_next[way])
        q = dt_at(way, 1, 0)
        arrive(("db", 1, way), dt.at[q, rows_of[1]], x_next[1 - way])
        hop(("db", 2, way), dt.at[q, sub_of[way]], x_next[way])
        hop(("dn", 1 + way), dt.at[q, rows_of[1]], near_y)
    for way in (1, 0):
        ref = dt.at[dt_at(way, 1, 1), rows_of[0]]
        arrive(("da", 1, 1, way), ref, x_next[1 - way])
        if way == 1:
            hop(("da", 2, 1), ref, x_next[way])
    for way in range(2):
        ref = dt.at[dt_at(way, 2, 0), sub_of[way]]
        arrive(("db", 2, way), ref, x_next[1 - way])
        hop(("dn", 3 + way), ref, near_y)
    for d in range(1, NQ):
        post(("w1", d), w_term.at[(rep + d) % NQ], w_in.at[d - 1], rep_peer(d))
    for s in range(2):
        arrive(("da", 2, s), dt.at[dt_at(s, 2, s), rows_of[0]], x_next[1 - s])
    arrive(("dn", 0), dt.at[dt_at(0, 0, 1), rows_of[1]], near_y)
    for way in range(2):
        arrive(("dn", 1 + way), dt.at[dt_at(way, 1, 1), rows_of[1]], near_y)
    for way in range(2):
        arrive(("dn", 3 + way), dt.at[dt_at(way, 2, 1), sub_of[way]], near_y)

    def backward(c):
        live = count_ref[0, c]
        picked = [
            dt[jnp.where(live > j, target_ref[0, 2 * c + j], NQ)] for j in range(2)
        ]
        return jnp.dot(
            jnp.concatenate(picked, axis=1), tile[pl.ds(2 * c, 2)].reshape(2 * T, T),
            preferred_element_type=F32,
        )

    base = {4: 0, 3: 2, 2: 6, 1: 10, 0: 14}
    count = {4: 2, 3: 4, 2: 4, 1: 4, 0: 2}

    def backward_group(t, core, store):
        def body(i, carry):
            way, s = i % 2, i // 2
            if t == 0 or t == NZ // 2:
                way, s = 0, i
            zt = (z + jnp.where(way == 0, t, NZ - t)) % NZ
            c = block(jnp.where(s == 0, 1 - yh, yh), zt, core)
            store(base[t] + i, backward(c))
            return carry

        lax.fori_loop(0, count[t], body, 0)

    def for_sib(t):
        def store(i, value):
            e_sib_out[i] = value.astype(BF16)

        backward_group(t, 1 - k, store)
        part = pl.ds(base[t], count[t])
        post(("es", t), e_sib_out.at[part], e_sib_in.at[part], sib)

    def for_own(t):
        def store(i, value):
            run[i] = value

        backward_group(t, k, store)

    def sib_in(t):
        part = pl.ds(base[t], count[t])
        arrive(("es", t), e_sib_in.at[part], sib)

    def chip_sum(i, h):
        rows = rows_of[h]
        return run[i, rows] + e_sib_in[i, rows].astype(F32)

    quarter = HALF // 2

    def far_sum_post(t):
        for way in range(1 if t in (0, FAR) else 2):
            o = 0 if t == FAR else 7 if t == 0 else 1 + 2 * (3 - t) + way
            ef_out[o] = chip_sum(base[t] + way, 1).astype(BF16)
            post(("ef", o), ef_out.at[o], ef_in.at[o], far_y)

    def low_sum(t, way):
        o = 0 if t == FAR else 7 if t == 0 else 1 + 2 * (3 - t) + way
        arrive(("ef", o), ef_in.at[o], far_y)
        i = base[t] + (1 if t in (0, FAR) else 2 + way)
        return chip_sum(i, 1) + ef_in[o].astype(F32)

    def ring_top(t, s):
        if t == FAR:
            ea_out[s] = chip_sum(base[t] + s, 0).astype(BF16)
            post(("ea", s), ea_out.at[s], ea_in.at[s], z_next[s])
            return
        for way in (1 - s, s):
            value = chip_sum(base[t] + 2 * s + way, 0)
            o = 2 + 4 * (3 - t) + 2 * s + way
            before = o - 4 if t < 3 else s if way == s else None
            if before is not None:
                arrive(("ea", before), ea_in.at[before], z_next[1 - way])
                value = value + ea_in[before].astype(F32)
            ea_out[o] = value.astype(BF16)
            post(("ea", o), ea_out.at[o], ea_in.at[o], z_next[way])

    def ring_low(t):
        if t == FAR:
            eb_out[0] = low_sum(t, 0).astype(BF16)
            for way in range(2):
                part = pl.ds(way * quarter, quarter)
                post(("eh", way), eb_out.at[0, part], eb_in.at[0, part], z_next[way])
            return
        for way in range(2):
            value = low_sum(t, way)
            o = 1 + 2 * (3 - t) + way
            if t == 3:
                part = pl.ds(way * quarter, quarter)
                arrive(("eh", way), eb_in.at[0, part], z_next[1 - way])
                more = value[way * quarter : (way + 1) * quarter] + eb_in[0, part].astype(F32)
                keep = value[(1 - way) * quarter : (2 - way) * quarter]
                eb_out[o, part] = more.astype(BF16)
                eb_out[o, pl.ds((1 - way) * quarter, quarter)] = keep.astype(BF16)
            else:
                arrive(("eb", o - 2), eb_in.at[o - 2], z_next[1 - way])
                eb_out[o] = (value + eb_in[o - 2].astype(F32)).astype(BF16)
            post(("eb", o), eb_out.at[o], eb_in.at[o], z_next[way])

    def sum_rep():
        for d in range(1, NQ):
            arrive(("w1", d), w_in.at[d - 1], rep_peer(NQ - d))
        total = w_term[rep].astype(F32)
        for d in range(1, NQ):
            total = total + w_in[d - 1].astype(F32)
        w_a[...] = total.reshape(NZ, 8, HALF)
        for i in range(3):
            post(("w2", i), w_a, w_b.at[i], group[i])

    def sum_group():
        for i in range(3):
            arrive(("w2", i), w_b.at[i], group[i])
        w_c[...] = (w_a[...] + w_b[0]) + (w_b[1] + w_b[2])
        for d in range(1, NZ):
            post(("w4", d), w_c.at[(z + d) % NZ], w_z_in.at[d - 1], z_peer(d))

    def sum_z():
        for d in range(1, NZ):
            arrive(("w4", d), w_z_in.at[d - 1], z_peer(NZ - d))
        total = w_c[z]
        for d in range(1, NZ):
            total = total + w_z_in[d - 1]
        w_e[z] = total
        for d in range(1, NZ):
            post(("w5", d), w_e.at[z], w_e.at[z], z_peer(d))

    def spread_rep():
        for d in range(1, NZ):
            arrive(("w5", d), w_e.at[(z + NZ - d) % NZ], z_peer(NZ - d))
        w_all[rep] = w_e[...].reshape(NZ * 8, HALF).astype(BF16)
        for d in range(1, NQ):
            post(("w6", d), w_all.at[rep], w_all.at[rep], rep_peer(d))

    for_sib(4)
    for_own(4)
    for_sib(3)
    sib_in(4)
    far_sum_post(4)
    ring_top(4, 0)
    ring_top(4, 1)
    for_own(3)
    sib_in(3)
    far_sum_post(3)
    for_sib(2)
    ring_top(3, 0)
    ring_top(3, 1)
    sum_rep()
    ring_low(4)
    for_own(2)
    sib_in(2)
    far_sum_post(2)
    for_sib(1)
    ring_top(2, 0)
    ring_top(2, 1)
    sum_group()
    ring_low(3)
    for_own(1)
    sib_in(1)
    far_sum_post(1)
    for_sib(0)
    for_own(0)
    ring_top(1, 0)
    sum_z()
    ring_top(1, 1)
    sib_in(0)
    far_sum_post(0)
    ring_low(2)
    spread_rep()
    ring_low(1)
    for s in range(2):
        i = 10 + 2 * s
        for way in range(2):
            arrive(("ea", i + way), ea_in.at[i + way], z_next[1 - way])
        total = (
            chip_sum(base[0] + s, 0) + ea_in[i].astype(F32) + ea_in[i + 1].astype(F32)
        )
        if s == 0:
            ey_out[...] = total.astype(BF16)
            post("ey", ey_out, ey_in, far_y)
        else:
            run[0, rows_of[0]] = total
    low_total = low_sum(0, 0)
    for way in range(2):
        arrive(("eb", 5 + way), eb_in.at[5 + way], z_next[1 - way])
    low_total = low_total + eb_in[5].astype(F32) + eb_in[6].astype(F32)
    fgrad_ref[:, HALF:] = low_total.T.astype(BF16)
    for d in range(1, NQ):
        arrive(("w6", d), w_all.at[(rep + NQ - d) % NQ], rep_peer(NQ - d))
    for q in range(NQ):
        done = w_all[q].astype(F32)
        for n in range(NZ):
            up, side = 32 * q + 8 * (n // 2), HALF * (n % 2)
            wgrad_ref[up : up + 8, side : side + HALF] = done[8 * n : 8 * n + 8]
    arrive("ey", ey_in, far_y)
    fgrad_ref[:, :HALF] = (run[0, rows_of[0]] + ey_in[...].astype(F32)).T.astype(BF16)
    for copy in started:
        copy.wait_send()


def local(features, tiles, tile_target, tile_count, weight, cotangent):
    vmem = pl.BlockSpec(memory_space=pltpu.VMEM)
    hbm = pl.BlockSpec(memory_space=pltpu.HBM)

    def buf(*shape, dtype=BF16):
        return pltpu.VMEM(shape, dtype)

    return pl.pallas_call(
        kernel,
        out_shape=(
            jax.ShapeDtypeStruct((T, T), BF16),
            jax.ShapeDtypeStruct((T, T), BF16),
            jax.ShapeDtypeStruct((T, T), F32),
        ),
        in_specs=[hbm] * 6,
        out_specs=(vmem, vmem, vmem),
        scratch_shapes=[
            pltpu.SMEM((1, SLOTS), jnp.int32),
            pltpu.SMEM((1, NC), jnp.int32),
            buf(T, T),
            buf(T, T),
            buf(2, NC, T, HALF),
            buf(SLOTS, T, T),
            buf(SLOTS + 1, T, T, dtype=F32),
            pltpu.SMEM((NQ,), jnp.int32),
            buf(NQ + 1, T, T),
            buf(6, T, HALF),
            buf(6, T, HALF),
            buf(3, T, HALF),
            buf(3, T, HALF),
            buf(4, T, HALF),
            buf(4, T, HALF),
            buf(T, HALF),
            buf(T, HALF),
            buf(T, T, dtype=F32),
            buf(16, T, T),
            buf(16, T, T),
            buf(14, HALF, T),
            buf(14, HALF, T),
            buf(7, HALF, T),
            buf(7, HALF, T),
            buf(8, HALF, T),
            buf(8, HALF, T),
            buf(HALF, T),
            buf(HALF, T),
            buf(NQ, NZ * 8, HALF),
            buf(NQ - 1, NZ * 8, HALF),
            buf(NZ, 8, HALF, dtype=F32),
            buf(3, NZ, 8, HALF, dtype=F32),
            buf(NZ, 8, HALF, dtype=F32),
            buf(NZ - 1, 8, HALF, dtype=F32),
            buf(NZ, 8, HALF, dtype=F32),
            buf(NQ, NZ * 8, HALF),
            pltpu.SemaphoreType.DMA((TILE_PARTS,)),
            pltpu.SemaphoreType.DMA((6,)),
            pltpu.SemaphoreType.DMA((SENDS,)),
            pltpu.SemaphoreType.DMA((SENDS,)),
        ],
        compiler_params=pltpu.CompilerParams(
            collective_id=0, has_side_effects=True, vmem_limit_bytes=46 * 1024 * 1024
        ),
        name="graph_layer",
    )(*[
        pltpu.with_memory_space_constraint(value, pltpu.HBM)
        for value in (features, tiles, tile_target, tile_count, weight, cotangent)
    ])


def solution(mesh):
    return jax.shard_map(
        local,
        mesh=mesh,
        in_specs=(
            P(("row", "rep"), None),
            P(("row", "rep"), None, None),
            P(("row", "rep"), None),
            P(("row", "rep"), None),
            P(),
            P(("row", "rep"), None),
        ),
        out_specs=(P(("row", "rep"), None), P(("row", "rep"), None), P()),
        check_vma=False,
    )
```

```python
import jax
import jax.numpy as jnp
from jax import lax
from jax.experimental import pallas as pl
from jax.experimental.pallas import tpu as pltpu
from jax.sharding import PartitionSpec as P

MESH = pl.DeviceIdType.MESH
F32 = jnp.float32
BF16 = jnp.bfloat16
T = 256
HALF = 128
NZ = 8
NX = 4
NQ = 8
NC = 32
SLOTS = 64
TILE_PARTS = 8
SENDS = 192


def kernel(
    x_hbm, tiles_ref, target_hbm, count_hbm, w_hbm, ct_hbm,
    hidden_ref, fgrad_ref, wgrad_ref,
    target_ref, count_ref, w_ref, ct_ref, feat, tile, run, last_at, dt,
    ba_out, ba_in, bb_out, bb_in, bn_out, bn_in, by_out, by_in, b_keep,
    e_sib_out, e_sib_in, ea_out, ea_in, eb_out, eb_in, ef_out, ef_in, ey_out, ey_in,
    w_term, w_in, w_a, w_b, w_c, w_z_in, w_e, w_all,
    tile_sem, in_sem, snd, rcv,
):
    row, rep = lax.axis_index("row"), lax.axis_index("rep")
    k, z, yh = row % 2, (row // 2) % NZ, row // (2 * NZ)
    x, yl = rep // 2, rep % 2

    def block(yh_, z_, k_):
        return yh_ * (2 * NZ) + z_ * 2 + k_

    me = row
    sib = (block(yh, z, 1 - k), rep)
    far_y = (block(1 - yh, z, k), rep)
    group = [sib, far_y, (block(1 - yh, z, 1 - k), rep)]
    z_next = [(block(yh, (z + 1) % NZ, k), rep), (block(yh, (z + NZ - 1) % NZ, k), rep)]
    x_next = [(row, ((x + 1) % NX) * 2 + yl), (row, ((x + NX - 1) % NX) * 2 + yl)]
    near_y = (row, x * 2 + 1 - yl)

    def z_peer(d):
        return (block(yh, (z + d) % NZ, k), rep)

    def rep_peer(d):
        return (row, (rep + d) % NQ)

    number = {}
    started = []

    def sem_of(name):
        return number.setdefault(name, len(number))

    def post(name, src, dst, device):
        i = sem_of(name)
        copy = pltpu.make_async_remote_copy(
            src_ref=src, dst_ref=dst, send_sem=snd.at[i], recv_sem=rcv.at[i],
            device_id=device, device_id_type=MESH,
        )
        copy.start()
        started.append(copy)

    def drain(keep):
        while len(started) > keep:
            started.pop(0).wait_send()

    def arrive(name, dst, device):
        i = sem_of(name)
        pltpu.make_async_remote_copy(
            src_ref=dst, dst_ref=dst, send_sem=snd.at[i], recv_sem=rcv.at[i],
            device_id=device, device_id_type=MESH,
        ).wait_recv()

    inputs = [
        (x_hbm.at[:, pl.ds(0, HALF)], feat.at[0, me]),
        (x_hbm.at[:, pl.ds(HALF, HALF)], feat.at[1, me]),
        (target_hbm, target_ref),
        (count_hbm, count_ref),
        (w_hbm, w_ref),
        (ct_hbm, ct_ref),
    ]
    inputs = [
        pltpu.make_async_copy(src, dst, in_sem.at[i]) for i, (src, dst) in enumerate(inputs)
    ]
    for copy in inputs:
        copy.start()
    loads = []
    per = SLOTS // TILE_PARTS
    for i in range(TILE_PARTS):
        copy = pltpu.make_async_copy(
            tiles_ref.at[pl.ds(i * per, per)], tile.at[pl.ds(i * per, per)], tile_sem.at[i]
        )
        copy.start()
        loads.append(copy)

    barrier = pltpu.get_barrier_semaphore()
    peers = group + [z_peer(d) for d in range(1, NZ)] + [rep_peer(d) for d in range(1, NQ)]
    for peer in peers:
        pl.semaphore_signal(barrier, inc=1, device_id=peer, device_id_type=MESH)
    run[SLOTS] = jnp.zeros((T, T), F32)
    dt[NQ] = jnp.zeros((T, T), BF16)
    pl.semaphore_wait(barrier, len(peers))

    rows_of = [pl.ds(0, HALF), pl.ds(HALF, HALF)]
    FAR = NZ // 2

    def yh_of(s):
        return yh if s == 0 else 1 - yh

    def z_at(way, t):
        return (z + NZ - t) % NZ if way == 0 else (z + t) % NZ

    def tags(h, t, s):
        if t == 0:
            return [0]
        if t == FAR and h == 0:
            return [s]
        return [0, 1]

    def piece(h, t, s, tag, core, split):
        c = block(yh_of(s), z_at(tag, t), core)
        if split:
            return feat.at[h, c, rows_of[tag]]
        return feat.at[h, c]

    def forward(c, p, last):
        prod = jnp.dot(
            tile[pl.ds(2 * c, 2)].reshape(2 * T, T),
            jnp.concatenate([feat[0, c], feat[1, c]], axis=1),
            preferred_element_type=F32,
        )
        live = count_ref[0, c]
        for j in range(2):
            target = target_ref[0, 2 * c + j]
            before = jnp.int32(SLOTS)
            for q in range(NQ):
                before = jnp.where(target == q, last[q], before)
            run[2 * p + j] = prod[j * T : (j + 1) * T] + run[before]
            last = tuple(
                jnp.where((target == q) & (live > j), 2 * p + j, last[q]) for q in range(NQ)
            )
        return last

    state = {"last": (jnp.int32(SLOTS),) * NQ, "place": 0}

    def compute(t, s, core):
        start = state["place"]
        size = 1 if t in (0, FAR) else 2

        def body(i, last):
            zt = (z + jnp.where(i == 0, NZ - t, t)) % NZ
            return forward(block(yh_of(s), zt, core), start + i, last)

        state["last"] = lax.fori_loop(0, size, body, state["last"])
        state["place"] = start + size

    def split_at(h, t):
        return h == 1 and t == FAR

    def z_post(h, s, t, tag):
        ref = piece(h, t - 1, s, tag, k, split_at(h, t))
        post(("az", h, s, t, tag), ref, ref, z_next[tag])

    def sib_post(h, t, s, tag):
        ref = piece(h, t, s, tag, k, split_at(h, t))
        post(("as", h, t, s, tag), ref, ref, sib)

    def far_post(t, tag):
        ref = piece(1, t, 0, tag, k, split_at(1, t))
        post(("af", t, tag), ref, ref, far_y)

    def sib_wait(t, s):
        for h in range(2):
            for tag in tags(h, t, s):
                arrive(
                    ("as", h, t, s, tag), piece(h, t, s, tag, 1 - k, split_at(h, t)), sib
                )

    for copy in inputs[:2]:
        copy.wait()
    own = feat.at[0, me]
    post("ay", own, own, far_y)
    for h in range(2):
        for way in range(2):
            z_post(h, 0, 1, way)
    far_post(0, 0)
    for h in range(2):
        sib_post(h, 0, 0, 0)
    arrive("ay", piece(0, 0, 1, 0, k, False), far_y)
    for way in range(2):
        z_post(0, 1, 1, way)
    sib_post(0, 0, 1, 0)
    for copy in inputs[2:4] + loads:
        copy.wait()
    compute(0, 0, k)
    def z_step(h, s, t):
        for tag in tags(h, t, s):
            ref = piece(h, t, s, tag, k, split_at(h, t))
            arrive(("az", h, s, t, tag), ref, z_next[1 - tag])
            if t < FAR and tag in tags(h, t + 1, s):
                z_post(h, s, t + 1, tag)
            if h == 1:
                far_post(t, tag)
            sib_post(h, t, s, tag)

    def far_step(t):
        for tag in tags(1, t, 1):
            arrive(("af", t, tag), piece(1, t, 1, tag, k, split_at(1, t)), far_y)
            sib_post(1, t, 1, tag)

    for t in range(1, FAR + 3):
        if t <= FAR:
            z_step(1, 0, t)
            z_step(0, 0, t)
        if t == FAR + 1:
            far_step(FAR)
        if t >= 2:
            sib_wait(t - 2, 1)
            compute(t - 2, 1, 1 - k)
        if t - 1 <= FAR:
            sib_wait(t - 1, 0)
            compute(t - 1, 0, 1 - k)
        if t <= FAR:
            z_step(0, 1, t)
            far_step(t - 1)
            compute(t, 0, k)
        if t - 1 <= FAR:
            compute(t - 1, 1, k)
    for q in range(NQ):
        last_at[q] = state["last"][q]

    every = pl.ds(0, T)

    def partial(q, h):
        return run[last_at[q], :, h * HALF : (h + 1) * HALF]

    def q_at(way, t, s):
        return ((x + (t if way == 0 else NX - t)) % NX) * 2 + (1 - yl if s == 0 else yl)

    def near_post(i, q):
        bn_out[i] = partial(q, 1).astype(BF16)
        post(("bn", i), bn_out.at[i], bn_in.at[i], near_y)

    def a_post(i, value, way):
        ba_out[i] = value.astype(BF16)
        post(("ba", i), ba_out.at[i], ba_in.at[i], x_next[way])

    near_post(0, q_at(0, 2, 0))
    for s in range(2):
        a_post(s, partial(q_at(0, 2, s), 0), s)
    for way in range(2):
        near_post(1 + way, q_at(way, 1, 0))
    for s in range(2):
        way = 1 - s
        a_post(2 + 2 * s + way, partial(q_at(way, 1, s), 0), way)
    near_post(3, q_at(0, 0, 0))
    drain(8)
    for s in range(2):
        arrive(("ba", s), ba_in.at[s], x_next[1 - s])
        a_post(2 + 3 * s, partial(q_at(s, 1, s), 0) + ba_in[s].astype(F32), s)
    arrive(("bn", 0), bn_in.at[0], near_y)
    bb_out[0] = (partial(q_at(0, 2, 1), 1) + bn_in[0].astype(F32)).astype(BF16)
    for way in range(2):
        post(
            ("bh", way), bb_out.at[0, rows_of[way]], bb_in.at[0, rows_of[way]], x_next[way]
        )
    for way in range(2):
        arrive(("bn", 1 + way), bn_in.at[1 + way], near_y)
        arrive(("bh", way), bb_in.at[0, rows_of[way]], x_next[1 - way])
        value = partial(q_at(way, 1, 1), 1) + bn_in[1 + way].astype(F32)
        extra = bb_in[0, rows_of[way]].astype(F32)
        keep, more = slice((1 - way) * HALF, (2 - way) * HALF), slice(way * HALF, (1 + way) * HALF)
        bb_out[1 + way, rows_of[1 - way]] = value[keep].astype(BF16)
        bb_out[1 + way, rows_of[way]] = (value[more] + extra).astype(BF16)
        post(("bb", way), bb_out.at[1 + way], bb_in.at[1 + way], x_next[way])
    for s in range(2):
        for way in range(2):
            i = 2 + 2 * s + way
            arrive(("ba", i), ba_in.at[i], x_next[1 - way])
        total = (
            partial(q_at(0, 0, s), 0)
            + ba_in[2 + 2 * s].astype(F32) + ba_in[3 + 2 * s].astype(F32)
        )
        if s == 0:
            by_out[...] = total.astype(BF16)
            post("by", by_out, by_in, near_y)
        else:
            b_keep[:, :HALF] = total
    arrive(("bn", 3), bn_in.at[3], near_y)
    for way in range(2):
        arrive(("bb", way), bb_in.at[1 + way], x_next[1 - way])
    b_keep[:, HALF:] = (
        partial(q_at(0, 0, 1), 1) + bn_in[3].astype(F32)
        + bb_in[1].astype(F32) + bb_in[2].astype(F32)
    )
    arrive("by", by_in, near_y)
    b_keep[:, :HALF] = b_keep[:, :HALF] + by_in[...].astype(F32)
    agg = b_keep[...].astype(BF16)

    for copy in inputs[4:]:
        copy.wait()
    pre = jnp.dot(agg, w_ref[...], preferred_element_type=F32)
    sigma = jax.nn.sigmoid(pre)
    grad_pre = (ct_ref[...].astype(F32) * sigma * (1.0 + pre * (1.0 - sigma))).astype(BF16)
    dt[rep] = lax.dot_general(
        w_ref[...], grad_pre, (((1,), (1,)), ((), ())), preferred_element_type=F32
    ).astype(BF16)

    sub_of = [pl.ds(HALF, HALF // 2), pl.ds(HALF + HALF // 2, HALF // 2)]

    def dt_at(way, t, s):
        return ((x + (NX - t if way == 0 else t)) % NX) * 2 + (yl if s == 0 else 1 - yl)

    def hop(name, ref, device):
        post(name, ref, ref, device)

    top, low = dt.at[rep, rows_of[0]], dt.at[rep, rows_of[1]]
    hop("dy", top, near_y)
    for way in range(2):
        hop(("da", 1, 0, way), top, x_next[way])
        hop(("db", 1, way), low, x_next[way])
    hop(("dn", 0), low, near_y)
    hidden_ref[...] = (pre * sigma).astype(BF16)
    near = dt.at[dt_at(0, 0, 1), rows_of[0]]
    arrive("dy", near, near_y)
    for way in range(2):
        hop(("da", 1, 1, way), near, x_next[way])
    term = lax.dot_general(agg, grad_pre, (((0,), (0,)), ((), ())), preferred_element_type=F32)
    for q in range(NQ):
        pieces = []
        for n in range(NZ):
            up, side = 32 * q + 8 * (n // 2), HALF * (n % 2)
            pieces.append(term[up : up + 8, side : side + HALF])
        w_term[q] = jnp.concatenate(pieces, axis=0).astype(BF16)

    drain(8)
    for way in range(2):
        ref = dt.at[dt_at(way, 1, 0), rows_of[0]]
        arrive(("da", 1, 0, way), ref, x_next[1 - way])
        if way == 0:
            hop(("da", 2, 0), ref, x_next[way])
        q = dt_at(way, 1, 0)
        arrive(("db", 1, way), dt.at[q, rows_of[1]], x_next[1 - way])
        hop(("db", 2, way), dt.at[q, sub_of[way]], x_next[way])
        hop(("dn", 1 + way), dt.at[q, rows_of[1]], near_y)
    for way in (1, 0):
        ref = dt.at[dt_at(way, 1, 1), rows_of[0]]
        arrive(("da", 1, 1, way), ref, x_next[1 - way])
        if way == 1:
            hop(("da", 2, 1), ref, x_next[way])
    for way in range(2):
        ref = dt.at[dt_at(way, 2, 0), sub_of[way]]
        arrive(("db", 2, way), ref, x_next[1 - way])
        hop(("dn", 3 + way), ref, near_y)
    for d in range(1, NQ):
        post(("w1", d), w_term.at[(rep + d) % NQ], w_in.at[d - 1], rep_peer(d))
    for s in range(2):
        arrive(("da", 2, s), dt.at[dt_at(s, 2, s), rows_of[0]], x_next[1 - s])
    arrive(("dn", 0), dt.at[dt_at(0, 0, 1), rows_of[1]], near_y)
    for way in range(2):
        arrive(("dn", 1 + way), dt.at[dt_at(way, 1, 1), rows_of[1]], near_y)
    for way in range(2):
        arrive(("dn", 3 + way), dt.at[dt_at(way, 2, 1), sub_of[way]], near_y)

    def backward(c):
        live = count_ref[0, c]
        picked = [
            dt[jnp.where(live > j, target_ref[0, 2 * c + j], NQ)] for j in range(2)
        ]
        return jnp.dot(
            jnp.concatenate(picked, axis=1), tile[pl.ds(2 * c, 2)].reshape(2 * T, T),
            preferred_element_type=F32,
        )

    base = {4: 0, 3: 2, 2: 6, 1: 10, 0: 14}
    count = {4: 2, 3: 4, 2: 4, 1: 4, 0: 2}

    def backward_group(t, core, store):
        def body(i, carry):
            way, s = i % 2, i // 2
            if t == 0 or t == NZ // 2:
                way, s = 0, i
            zt = (z + jnp.where(way == 0, t, NZ - t)) % NZ
            c = block(jnp.where(s == 0, 1 - yh, yh), zt, core)
            store(base[t] + i, backward(c))
            return carry

        lax.fori_loop(0, count[t], body, 0)

    def for_sib(t):
        def store(i, value):
            e_sib_out[i] = value.astype(BF16)

        backward_group(t, 1 - k, store)
        part = pl.ds(base[t], count[t])
        post(("es", t), e_sib_out.at[part], e_sib_in.at[part], sib)

    def for_own(t):
        def store(i, value):
            run[i] = value

        backward_group(t, k, store)

    def sib_in(t):
        part = pl.ds(base[t], count[t])
        arrive(("es", t), e_sib_in.at[part], sib)

    def chip_sum(i, h):
        rows = rows_of[h]
        return run[i, rows] + e_sib_in[i, rows].astype(F32)

    quarter = HALF // 2

    def far_sum_post(t):
        for way in range(1 if t in (0, FAR) else 2):
            o = 0 if t == FAR else 7 if t == 0 else 1 + 2 * (3 - t) + way
            ef_out[o] = chip_sum(base[t] + way, 1).astype(BF16)
            post(("ef", o), ef_out.at[o], ef_in.at[o], far_y)

    def low_sum(t, way):
        o = 0 if t == FAR else 7 if t == 0 else 1 + 2 * (3 - t) + way
        arrive(("ef", o), ef_in.at[o], far_y)
        i = base[t] + (1 if t in (0, FAR) else 2 + way)
        return chip_sum(i, 1) + ef_in[o].astype(F32)

    def ring_top(t, s):
        if t == FAR:
            ea_out[s] = chip_sum(base[t] + s, 0).astype(BF16)
            post(("ea", s), ea_out.at[s], ea_in.at[s], z_next[s])
            return
        for way in (1 - s, s):
            value = chip_sum(base[t] + 2 * s + way, 0)
            o = 2 + 4 * (3 - t) + 2 * s + way
            before = o - 4 if t < 3 else s if way == s else None
            if before is not None:
                arrive(("ea", before), ea_in.at[before], z_next[1 - way])
                value = value + ea_in[before].astype(F32)
            ea_out[o] = value.astype(BF16)
            post(("ea", o), ea_out.at[o], ea_in.at[o], z_next[way])

    def ring_low(t):
        if t == FAR:
            eb_out[0] = low_sum(t, 0).astype(BF16)
            for way in range(2):
                part = pl.ds(way * quarter, quarter)
                post(("eh", way), eb_out.at[0, part], eb_in.at[0, part], z_next[way])
            return
        for way in range(2):
            value = low_sum(t, way)
            o = 1 + 2 * (3 - t) + way
            if t == 3:
                part = pl.ds(way * quarter, quarter)
                arrive(("eh", way), eb_in.at[0, part], z_next[1 - way])
                more = value[way * quarter : (way + 1) * quarter] + eb_in[0, part].astype(F32)
                keep = value[(1 - way) * quarter : (2 - way) * quarter]
                eb_out[o, part] = more.astype(BF16)
                eb_out[o, pl.ds((1 - way) * quarter, quarter)] = keep.astype(BF16)
            else:
                arrive(("eb", o - 2), eb_in.at[o - 2], z_next[1 - way])
                eb_out[o] = (value + eb_in[o - 2].astype(F32)).astype(BF16)
            post(("eb", o), eb_out.at[o], eb_in.at[o], z_next[way])

    def sum_rep():
        for d in range(1, NQ):
            arrive(("w1", d), w_in.at[d - 1], rep_peer(NQ - d))
        total = w_term[rep].astype(F32)
        for d in range(1, NQ):
            total = total + w_in[d - 1].astype(F32)
        w_a[...] = total.reshape(NZ, 8, HALF)
        for i in range(3):
            post(("w2", i), w_a, w_b.at[i], group[i])

    def sum_group():
        for i in range(3):
            arrive(("w2", i), w_b.at[i], group[i])
        w_c[...] = (w_a[...] + w_b[0]) + (w_b[1] + w_b[2])
        for d in range(1, NZ):
            post(("w4", d), w_c.at[(z + d) % NZ], w_z_in.at[d - 1], z_peer(d))

    def sum_z():
        for d in range(1, NZ):
            arrive(("w4", d), w_z_in.at[d - 1], z_peer(NZ - d))
        total = w_c[z]
        for d in range(1, NZ):
            total = total + w_z_in[d - 1]
        w_e[z] = total
        for d in range(1, NZ):
            post(("w5", d), w_e.at[z], w_e.at[z], z_peer(d))

    def spread_rep():
        for d in range(1, NZ):
            arrive(("w5", d), w_e.at[(z + NZ - d) % NZ], z_peer(NZ - d))
        w_all[rep] = w_e[...].reshape(NZ * 8, HALF).astype(BF16)
        for d in range(1, NQ):
            post(("w6", d), w_all.at[rep], w_all.at[rep], rep_peer(d))

    for_sib(4)
    for_own(4)
    for_sib(3)
    sib_in(4)
    far_sum_post(4)
    ring_top(4, 0)
    ring_top(4, 1)
    for_own(3)
    sib_in(3)
    far_sum_post(3)
    drain(9)
    for_sib(2)
    ring_top(3, 0)
    ring_top(3, 1)
    sum_rep()
    ring_low(4)
    for_own(2)
    sib_in(2)
    far_sum_post(2)
    for_sib(1)
    ring_top(2, 0)
    ring_top(2, 1)
    sum_group()
    ring_low(3)
    drain(12)
    for_own(1)
    sib_in(1)
    far_sum_post(1)
    for_sib(0)
    for_own(0)
    ring_top(1, 0)
    sum_z()
    ring_top(1, 1)
    sib_in(0)
    far_sum_post(0)
    drain(16)
    ring_low(2)
    spread_rep()
    ring_low(1)
    for s in range(2):
        i = 10 + 2 * s
        for way in range(2):
            arrive(("ea", i + way), ea_in.at[i + way], z_next[1 - way])
        total = (
            chip_sum(base[0] + s, 0) + ea_in[i].astype(F32) + ea_in[i + 1].astype(F32)
        )
        if s == 0:
            ey_out[...] = total.astype(BF16)
            post("ey", ey_out, ey_in, far_y)
        else:
            run[0, rows_of[0]] = total
    drain(12)
    low_total = low_sum(0, 0)
    for way in range(2):
        arrive(("eb", 5 + way), eb_in.at[5 + way], z_next[1 - way])
    low_total = low_total + eb_in[5].astype(F32) + eb_in[6].astype(F32)
    fgrad_ref[:, HALF:] = low_total.T.astype(BF16)
    for d in range(1, NQ):
        arrive(("w6", d), w_all.at[(rep + NQ - d) % NQ], rep_peer(NQ - d))
    for q in range(NQ):
        done = w_all[q].astype(F32)
        for n in range(NZ):
            up, side = 32 * q + 8 * (n // 2), HALF * (n % 2)
            wgrad_ref[up : up + 8, side : side + HALF] = done[8 * n : 8 * n + 8]
    arrive("ey", ey_in, far_y)
    fgrad_ref[:, :HALF] = (run[0, rows_of[0]] + ey_in[...].astype(F32)).T.astype(BF16)
    drain(0)


def local(features, tiles, tile_target, tile_count, weight, cotangent):
    vmem = pl.BlockSpec(memory_space=pltpu.VMEM)
    hbm = pl.BlockSpec(memory_space=pltpu.HBM)

    def buf(*shape, dtype=BF16):
        return pltpu.VMEM(shape, dtype)

    return pl.pallas_call(
        kernel,
        out_shape=(
            jax.ShapeDtypeStruct((T, T), BF16),
            jax.ShapeDtypeStruct((T, T), BF16),
            jax.ShapeDtypeStruct((T, T), F32),
        ),
        in_specs=[hbm] * 6,
        out_specs=(vmem, vmem, vmem),
        scratch_shapes=[
            pltpu.SMEM((1, SLOTS), jnp.int32),
            pltpu.SMEM((1, NC), jnp.int32),
            buf(T, T),
            buf(T, T),
            buf(2, NC, T, HALF),
            buf(SLOTS, T, T),
            buf(SLOTS + 1, T, T, dtype=F32),
            pltpu.SMEM((NQ,), jnp.int32),
            buf(NQ + 1, T, T),
            buf(6, T, HALF),
            buf(6, T, HALF),
            buf(3, T, HALF),
            buf(3, T, HALF),
            buf(4, T, HALF),
            buf(4, T, HALF),
            buf(T, HALF),
            buf(T, HALF),
            buf(T, T, dtype=F32),
            buf(16, T, T),
            buf(16, T, T),
            buf(14, HALF, T),
            buf(14, HALF, T),
            buf(7, HALF, T),
            buf(7, HALF, T),
            buf(8, HALF, T),
            buf(8, HALF, T),
            buf(HALF, T),
            buf(HALF, T),
            buf(NQ, NZ * 8, HALF),
            buf(NQ - 1, NZ * 8, HALF),
            buf(NZ, 8, HALF, dtype=F32),
            buf(3, NZ, 8, HALF, dtype=F32),
            buf(NZ, 8, HALF, dtype=F32),
            buf(NZ - 1, 8, HALF, dtype=F32),
            buf(NZ, 8, HALF, dtype=F32),
            buf(NQ, NZ * 8, HALF),
            pltpu.SemaphoreType.DMA((TILE_PARTS,)),
            pltpu.SemaphoreType.DMA((6,)),
            pltpu.SemaphoreType.DMA((SENDS,)),
            pltpu.SemaphoreType.DMA((SENDS,)),
        ],
        compiler_params=pltpu.CompilerParams(
            collective_id=0, has_side_effects=True, vmem_limit_bytes=46 * 1024 * 1024
        ),
        name="graph_layer",
    )(*[
        pltpu.with_memory_space_constraint(value, pltpu.HBM)
        for value in (features, tiles, tile_target, tile_count, weight, cotangent)
    ])


def solution(mesh):
    return jax.shard_map(
        local,
        mesh=mesh,
        in_specs=(
            P(("row", "rep"), None),
            P(("row", "rep"), None, None),
            P(("row", "rep"), None),
            P(("row", "rep"), None),
            P(),
            P(("row", "rep"), None),
        ),
        out_specs=(P(("row", "rep"), None), P(("row", "rep"), None), P()),
        check_vma=False,
    )
```

```python
import jax
import jax.numpy as jnp
from jax import lax
from jax.experimental import pallas as pl
from jax.experimental.pallas import tpu as pltpu
from jax.sharding import PartitionSpec as P

MESH = pl.DeviceIdType.MESH
F32 = jnp.float32
BF16 = jnp.bfloat16
T = 256
HALF = 128
NZ = 8
NX = 4
NQ = 8
NC = 32
SLOTS = 64
TILE_PARTS = 8
SENDS = 192


def kernel(
    x_hbm, tiles_ref, target_hbm, count_hbm, w_hbm, ct_hbm,
    hidden_ref, fgrad_ref, wgrad_ref,
    target_ref, count_ref, w_ref, ct_ref, feat, tile, run, last_at, dt,
    ba_out, ba_in, bb_out, bb_in, bn_out, bn_in, by_out, by_in, b_keep,
    e_sib_out, e_sib_in, ea_out, ea_in, eb_out, eb_in, ef_out, ef_in, ey_out, ey_in,
    w_term, w_in, w_a, w_b, w_c, w_z_in, w_e, w_all,
    tile_sem, in_sem, snd, rcv,
):
    row, rep = lax.axis_index("row"), lax.axis_index("rep")
    k, z, yh = row % 2, (row // 2) % NZ, row // (2 * NZ)
    x, yl = rep // 2, rep % 2

    def block(yh_, z_, k_):
        return yh_ * (2 * NZ) + z_ * 2 + k_

    me = row
    sib = (block(yh, z, 1 - k), rep)
    far_y = (block(1 - yh, z, k), rep)
    group = [sib, far_y, (block(1 - yh, z, 1 - k), rep)]
    z_next = [(block(yh, (z + 1) % NZ, k), rep), (block(yh, (z + NZ - 1) % NZ, k), rep)]
    x_next = [(row, ((x + 1) % NX) * 2 + yl), (row, ((x + NX - 1) % NX) * 2 + yl)]
    near_y = (row, x * 2 + 1 - yl)

    def z_peer(d):
        return (block(yh, (z + d) % NZ, k), rep)

    def rep_peer(d):
        return (row, (rep + d) % NQ)

    number = {}
    started = []

    def sem_of(name):
        return number.setdefault(name, len(number))

    def post(name, src, dst, device):
        i = sem_of(name)
        copy = pltpu.make_async_remote_copy(
            src_ref=src, dst_ref=dst, send_sem=snd.at[i], recv_sem=rcv.at[i],
            device_id=device, device_id_type=MESH,
        )
        copy.start()
        started.append(copy)

    def drain(keep):
        while len(started) > keep:
            started.pop(0).wait_send()

    def arrive(name, dst, device):
        i = sem_of(name)
        pltpu.make_async_remote_copy(
            src_ref=dst, dst_ref=dst, send_sem=snd.at[i], recv_sem=rcv.at[i],
            device_id=device, device_id_type=MESH,
        ).wait_recv()

    inputs = [
        (x_hbm.at[:, pl.ds(0, HALF)], feat.at[0, me]),
        (x_hbm.at[:, pl.ds(HALF, HALF)], feat.at[1, me]),
        (target_hbm, target_ref),
        (count_hbm, count_ref),
        (w_hbm, w_ref),
        (ct_hbm, ct_ref),
    ]
    inputs = [
        pltpu.make_async_copy(src, dst, in_sem.at[i]) for i, (src, dst) in enumerate(inputs)
    ]
    for copy in inputs:
        copy.start()
    loads = []
    per = SLOTS // TILE_PARTS
    for i in range(TILE_PARTS):
        copy = pltpu.make_async_copy(
            tiles_ref.at[pl.ds(i * per, per)], tile.at[pl.ds(i * per, per)], tile_sem.at[i]
        )
        copy.start()
        loads.append(copy)

    barrier = pltpu.get_barrier_semaphore()
    peers = group + [z_peer(d) for d in range(1, NZ)] + [rep_peer(d) for d in range(1, NQ)]
    for peer in peers:
        pl.semaphore_signal(barrier, inc=1, device_id=peer, device_id_type=MESH)
    run[SLOTS] = jnp.zeros((T, T), F32)
    dt[NQ] = jnp.zeros((T, T), BF16)
    pl.semaphore_wait(barrier, len(peers))

    rows_of = [pl.ds(0, HALF), pl.ds(HALF, HALF)]
    FAR = NZ // 2

    def yh_of(s):
        return yh if s == 0 else 1 - yh

    def z_at(way, t):
        return (z + NZ - t) % NZ if way == 0 else (z + t) % NZ

    def tags(h, t, s):
        if t == 0:
            return [0]
        if t == FAR and h == 0:
            return [s]
        return [0, 1]

    def piece(h, t, s, tag, core, split):
        c = block(yh_of(s), z_at(tag, t), core)
        if split:
            return feat.at[h, c, rows_of[tag]]
        return feat.at[h, c]

    def forward(c, p, last):
        prod = jnp.dot(
            tile[pl.ds(2 * c, 2)].reshape(2 * T, T),
            jnp.concatenate([feat[0, c], feat[1, c]], axis=1),
            preferred_element_type=F32,
        )
        live = count_ref[0, c]
        for j in range(2):
            target = target_ref[0, 2 * c + j]
            before = jnp.int32(SLOTS)
            for q in range(NQ):
                before = jnp.where(target == q, last[q], before)
            run[2 * p + j] = prod[j * T : (j + 1) * T] + run[before]
            last = tuple(
                jnp.where((target == q) & (live > j), 2 * p + j, last[q]) for q in range(NQ)
            )
        return last

    state = {"last": (jnp.int32(SLOTS),) * NQ, "place": 0}

    def compute(t, s, core):
        start = state["place"]
        size = 1 if t in (0, FAR) else 2

        def body(i, last):
            zt = (z + jnp.where(i == 0, NZ - t, t)) % NZ
            return forward(block(yh_of(s), zt, core), start + i, last)

        state["last"] = lax.fori_loop(0, size, body, state["last"])
        state["place"] = start + size

    def split_at(h, t):
        return h == 1 and t == FAR

    def z_post(h, s, t, tag):
        ref = piece(h, t - 1, s, tag, k, split_at(h, t))
        post(("az", h, s, t, tag), ref, ref, z_next[tag])

    def sib_post(h, t, s, tag):
        ref = piece(h, t, s, tag, k, split_at(h, t))
        post(("as", h, t, s, tag), ref, ref, sib)

    def far_post(t, tag):
        ref = piece(1, t, 0, tag, k, split_at(1, t))
        post(("af", t, tag), ref, ref, far_y)

    def sib_wait(t, s):
        for h in range(2):
            for tag in tags(h, t, s):
                arrive(
                    ("as", h, t, s, tag), piece(h, t, s, tag, 1 - k, split_at(h, t)), sib
                )

    for copy in inputs[:2]:
        copy.wait()
    own = feat.at[0, me]
    post("ay", own, own, far_y)
    for h in range(2):
        for way in range(2):
            z_post(h, 0, 1, way)
    far_post(0, 0)
    for h in range(2):
        sib_post(h, 0, 0, 0)
    arrive("ay", piece(0, 0, 1, 0, k, False), far_y)
    for way in range(2):
        z_post(0, 1, 1, way)
    sib_post(0, 0, 1, 0)
    for copy in inputs[2:4] + loads:
        copy.wait()
    compute(0, 0, k)
    def z_step(h, s, t):
        for tag in tags(h, t, s):
            ref = piece(h, t, s, tag, k, split_at(h, t))
            arrive(("az", h, s, t, tag), ref, z_next[1 - tag])
            if t < FAR and tag in tags(h, t + 1, s):
                z_post(h, s, t + 1, tag)
            if h == 1:
                far_post(t, tag)
            sib_post(h, t, s, tag)

    def far_step(t):
        for tag in tags(1, t, 1):
            arrive(("af", t, tag), piece(1, t, 1, tag, k, split_at(1, t)), far_y)
            sib_post(1, t, 1, tag)

    for t in range(1, FAR + 3):
        if t <= FAR:
            z_step(1, 0, t)
            z_step(0, 0, t)
        if t >= 2:
            sib_wait(t - 2, 1)
            compute(t - 2, 1, 1 - k)
        if t == FAR + 1:
            far_step(FAR)
        if t - 1 <= FAR:
            sib_wait(t - 1, 0)
            compute(t - 1, 0, 1 - k)
        if t <= FAR:
            z_step(0, 1, t)
            far_step(t - 1)
            compute(t, 0, k)
        if t - 1 <= FAR:
            compute(t - 1, 1, k)
    for q in range(NQ):
        last_at[q] = state["last"][q]

    every = pl.ds(0, T)

    def partial(q, h):
        return run[last_at[q], :, h * HALF : (h + 1) * HALF]

    def q_at(way, t, s):
        return ((x + (t if way == 0 else NX - t)) % NX) * 2 + (1 - yl if s == 0 else yl)

    def near_post(i, q):
        bn_out[i] = partial(q, 1).astype(BF16)
        post(("bn", i), bn_out.at[i], bn_in.at[i], near_y)

    def a_post(i, value, way):
        ba_out[i] = value.astype(BF16)
        post(("ba", i), ba_out.at[i], ba_in.at[i], x_next[way])

    near_post(0, q_at(0, 2, 0))
    for s in range(2):
        a_post(s, partial(q_at(0, 2, s), 0), s)
    for way in range(2):
        near_post(1 + way, q_at(way, 1, 0))
    for s in range(2):
        way = 1 - s
        a_post(2 + 2 * s + way, partial(q_at(way, 1, s), 0), way)
    near_post(3, q_at(0, 0, 0))
    drain(8)
    for s in range(2):
        arrive(("ba", s), ba_in.at[s], x_next[1 - s])
        a_post(2 + 3 * s, partial(q_at(s, 1, s), 0) + ba_in[s].astype(F32), s)
    arrive(("bn", 0), bn_in.at[0], near_y)
    bb_out[0] = (partial(q_at(0, 2, 1), 1) + bn_in[0].astype(F32)).astype(BF16)
    for way in range(2):
        post(
            ("bh", way), bb_out.at[0, rows_of[way]], bb_in.at[0, rows_of[way]], x_next[way]
        )
    for way in range(2):
        arrive(("bn", 1 + way), bn_in.at[1 + way], near_y)
        arrive(("bh", way), bb_in.at[0, rows_of[way]], x_next[1 - way])
        value = partial(q_at(way, 1, 1), 1) + bn_in[1 + way].astype(F32)
        extra = bb_in[0, rows_of[way]].astype(F32)
        keep, more = slice((1 - way) * HALF, (2 - way) * HALF), slice(way * HALF, (1 + way) * HALF)
        bb_out[1 + way, rows_of[1 - way]] = value[keep].astype(BF16)
        bb_out[1 + way, rows_of[way]] = (value[more] + extra).astype(BF16)
        post(("bb", way), bb_out.at[1 + way], bb_in.at[1 + way], x_next[way])
    for s in range(2):
        for way in range(2):
            i = 2 + 2 * s + way
            arrive(("ba", i), ba_in.at[i], x_next[1 - way])
        total = (
            partial(q_at(0, 0, s), 0)
            + ba_in[2 + 2 * s].astype(F32) + ba_in[3 + 2 * s].astype(F32)
        )
        if s == 0:
            by_out[...] = total.astype(BF16)
            post("by", by_out, by_in, near_y)
        else:
            b_keep[:, :HALF] = total
    arrive(("bn", 3), bn_in.at[3], near_y)
    for way in range(2):
        arrive(("bb", way), bb_in.at[1 + way], x_next[1 - way])
    b_keep[:, HALF:] = (
        partial(q_at(0, 0, 1), 1) + bn_in[3].astype(F32)
        + bb_in[1].astype(F32) + bb_in[2].astype(F32)
    )
    arrive("by", by_in, near_y)
    b_keep[:, :HALF] = b_keep[:, :HALF] + by_in[...].astype(F32)
    agg = b_keep[...].astype(BF16)

    for copy in inputs[4:]:
        copy.wait()
    pre = jnp.dot(agg, w_ref[...], preferred_element_type=F32)
    sigma = jax.nn.sigmoid(pre)
    grad_pre = (ct_ref[...].astype(F32) * sigma * (1.0 + pre * (1.0 - sigma))).astype(BF16)
    dt[rep] = lax.dot_general(
        w_ref[...], grad_pre, (((1,), (1,)), ((), ())), preferred_element_type=F32
    ).astype(BF16)

    sub_of = [pl.ds(HALF, HALF // 2), pl.ds(HALF + HALF // 2, HALF // 2)]

    def dt_at(way, t, s):
        return ((x + (NX - t if way == 0 else t)) % NX) * 2 + (yl if s == 0 else 1 - yl)

    def hop(name, ref, device):
        post(name, ref, ref, device)

    top, low = dt.at[rep, rows_of[0]], dt.at[rep, rows_of[1]]
    hop("dy", top, near_y)
    for way in range(2):
        hop(("da", 1, 0, way), top, x_next[way])
        hop(("db", 1, way), low, x_next[way])
    hop(("dn", 0), low, near_y)
    hidden_ref[...] = (pre * sigma).astype(BF16)
    near = dt.at[dt_at(0, 0, 1), rows_of[0]]
    arrive("dy", near, near_y)
    for way in range(2):
        hop(("da", 1, 1, way), near, x_next[way])
    term = lax.dot_general(agg, grad_pre, (((0,), (0,)), ((), ())), preferred_element_type=F32)
    for q in range(NQ):
        pieces = []
        for n in range(NZ):
            up, side = 32 * q + 8 * (n // 2), HALF * (n % 2)
            pieces.append(term[up : up + 8, side : side + HALF])
        w_term[q] = jnp.concatenate(pieces, axis=0).astype(BF16)

    drain(8)
    for way in range(2):
        ref = dt.at[dt_at(way, 1, 0), rows_of[0]]
        arrive(("da", 1, 0, way), ref, x_next[1 - way])
        if way == 0:
            hop(("da", 2, 0), ref, x_next[way])
        q = dt_at(way, 1, 0)
        arrive(("db", 1, way), dt.at[q, rows_of[1]], x_next[1 - way])
        hop(("db", 2, way), dt.at[q, sub_of[way]], x_next[way])
        hop(("dn", 1 + way), dt.at[q, rows_of[1]], near_y)
    for way in (1, 0):
        ref = dt.at[dt_at(way, 1, 1), rows_of[0]]
        arrive(("da", 1, 1, way), ref, x_next[1 - way])
        if way == 1:
            hop(("da", 2, 1), ref, x_next[way])
    for way in range(2):
        ref = dt.at[dt_at(way, 2, 0), sub_of[way]]
        arrive(("db", 2, way), ref, x_next[1 - way])
        hop(("dn", 3 + way), ref, near_y)
    for d in range(1, NQ):
        post(("w1", d), w_term.at[(rep + d) % NQ], w_in.at[d - 1], rep_peer(d))
    for s in range(2):
        arrive(("da", 2, s), dt.at[dt_at(s, 2, s), rows_of[0]], x_next[1 - s])
    arrive(("dn", 0), dt.at[dt_at(0, 0, 1), rows_of[1]], near_y)
    for way in range(2):
        arrive(("dn", 1 + way), dt.at[dt_at(way, 1, 1), rows_of[1]], near_y)
    for way in range(2):
        arrive(("dn", 3 + way), dt.at[dt_at(way, 2, 1), sub_of[way]], near_y)

    def backward(c):
        live = count_ref[0, c]
        picked = [
            dt[jnp.where(live > j, target_ref[0, 2 * c + j], NQ)] for j in range(2)
        ]
        return jnp.dot(
            jnp.concatenate(picked, axis=1), tile[pl.ds(2 * c, 2)].reshape(2 * T, T),
            preferred_element_type=F32,
        )

    base = {4: 0, 3: 2, 2: 6, 1: 10, 0: 14}
    count = {4: 2, 3: 4, 2: 4, 1: 4, 0: 2}

    def backward_group(t, core, store):
        def body(i, carry):
            way, s = i % 2, i // 2
            if t == 0 or t == NZ // 2:
                way, s = 0, i
            zt = (z + jnp.where(way == 0, t, NZ - t)) % NZ
            c = block(jnp.where(s == 0, 1 - yh, yh), zt, core)
            store(base[t] + i, backward(c))
            return carry

        lax.fori_loop(0, count[t], body, 0)

    def for_sib(t):
        def store(i, value):
            e_sib_out[i] = value.astype(BF16)

        backward_group(t, 1 - k, store)
        part = pl.ds(base[t], count[t])
        post(("es", t), e_sib_out.at[part], e_sib_in.at[part], sib)

    def for_own(t):
        def store(i, value):
            run[i] = value

        backward_group(t, k, store)

    def sib_in(t):
        part = pl.ds(base[t], count[t])
        arrive(("es", t), e_sib_in.at[part], sib)

    def chip_sum(i, h):
        rows = rows_of[h]
        return run[i, rows] + e_sib_in[i, rows].astype(F32)

    quarter = HALF // 2

    def far_sum_post(t):
        for way in range(1 if t in (0, FAR) else 2):
            o = 0 if t == FAR else 7 if t == 0 else 1 + 2 * (3 - t) + way
            ef_out[o] = chip_sum(base[t] + way, 1).astype(BF16)
            post(("ef", o), ef_out.at[o], ef_in.at[o], far_y)

    def low_sum(t, way):
        o = 0 if t == FAR else 7 if t == 0 else 1 + 2 * (3 - t) + way
        arrive(("ef", o), ef_in.at[o], far_y)
        i = base[t] + (1 if t in (0, FAR) else 2 + way)
        return chip_sum(i, 1) + ef_in[o].astype(F32)

    def ring_top(t, s):
        if t == FAR:
            ea_out[s] = chip_sum(base[t] + s, 0).astype(BF16)
            post(("ea", s), ea_out.at[s], ea_in.at[s], z_next[s])
            return
        for way in (1 - s, s):
            value = chip_sum(base[t] + 2 * s + way, 0)
            o = 2 + 4 * (3 - t) + 2 * s + way
            before = o - 4 if t < 3 else s if way == s else None
            if before is not None:
                arrive(("ea", before), ea_in.at[before], z_next[1 - way])
                value = value + ea_in[before].astype(F32)
            ea_out[o] = value.astype(BF16)
            post(("ea", o), ea_out.at[o], ea_in.at[o], z_next[way])

    def ring_low(t):
        if t == FAR:
            eb_out[0] = low_sum(t, 0).astype(BF16)
            for way in range(2):
                part = pl.ds(way * quarter, quarter)
                post(("eh", way), eb_out.at[0, part], eb_in.at[0, part], z_next[way])
            return
        for way in range(2):
            value = low_sum(t, way)
            o = 1 + 2 * (3 - t) + way
            if t == 3:
                part = pl.ds(way * quarter, quarter)
                arrive(("eh", way), eb_in.at[0, part], z_next[1 - way])
                more = value[way * quarter : (way + 1) * quarter] + eb_in[0, part].astype(F32)
                keep = value[(1 - way) * quarter : (2 - way) * quarter]
                eb_out[o, part] = more.astype(BF16)
                eb_out[o, pl.ds((1 - way) * quarter, quarter)] = keep.astype(BF16)
            else:
                arrive(("eb", o - 2), eb_in.at[o - 2], z_next[1 - way])
                eb_out[o] = (value + eb_in[o - 2].astype(F32)).astype(BF16)
            post(("eb", o), eb_out.at[o], eb_in.at[o], z_next[way])

    def sum_rep():
        for d in range(1, NQ):
            arrive(("w1", d), w_in.at[d - 1], rep_peer(NQ - d))
        total = w_term[rep].astype(F32)
        for d in range(1, NQ):
            total = total + w_in[d - 1].astype(F32)
        w_a[...] = total.reshape(NZ, 8, HALF)
        for i in range(3):
            post(("w2", i), w_a, w_b.at[i], group[i])

    def sum_group():
        for i in range(3):
            arrive(("w2", i), w_b.at[i], group[i])
        w_c[...] = (w_a[...] + w_b[0]) + (w_b[1] + w_b[2])
        for d in range(1, NZ):
            post(("w4", d), w_c.at[(z + d) % NZ], w_z_in.at[d - 1], z_peer(d))

    def sum_z():
        for d in range(1, NZ):
            arrive(("w4", d), w_z_in.at[d - 1], z_peer(NZ - d))
        total = w_c[z]
        for d in range(1, NZ):
            total = total + w_z_in[d - 1]
        w_e[z] = total
        for d in range(1, NZ):
            post(("w5", d), w_e.at[z], w_e.at[z], z_peer(d))

    def spread_rep():
        for d in range(1, NZ):
            arrive(("w5", d), w_e.at[(z + NZ - d) % NZ], z_peer(NZ - d))
        w_all[rep] = w_e[...].reshape(NZ * 8, HALF).astype(BF16)
        for d in range(1, NQ):
            post(("w6", d), w_all.at[rep], w_all.at[rep], rep_peer(d))

    for_sib(4)
    for_own(4)
    for_sib(3)
    sib_in(4)
    far_sum_post(4)
    ring_top(4, 0)
    ring_top(4, 1)
    for_own(3)
    sib_in(3)
    far_sum_post(3)
    drain(9)
    for_sib(2)
    ring_top(3, 0)
    ring_top(3, 1)
    sum_rep()
    ring_low(4)
    for_own(2)
    sib_in(2)
    far_sum_post(2)
    for_sib(1)
    ring_top(2, 0)
    ring_top(2, 1)
    sum_group()
    ring_low(3)
    drain(12)
    for_own(1)
    sib_in(1)
    far_sum_post(1)
    for_sib(0)
    for_own(0)
    ring_top(1, 0)
    sum_z()
    ring_top(1, 1)
    sib_in(0)
    far_sum_post(0)
    drain(16)
    ring_low(2)
    spread_rep()
    ring_low(1)
    for s in range(2):
        i = 10 + 2 * s
        for way in range(2):
            arrive(("ea", i + way), ea_in.at[i + way], z_next[1 - way])
        total = (
            chip_sum(base[0] + s, 0) + ea_in[i].astype(F32) + ea_in[i + 1].astype(F32)
        )
        if s == 0:
            ey_out[...] = total.astype(BF16)
            post("ey", ey_out, ey_in, far_y)
        else:
            run[0, rows_of[0]] = total
    drain(12)
    low_total = low_sum(0, 0)
    for way in range(2):
        arrive(("eb", 5 + way), eb_in.at[5 + way], z_next[1 - way])
    low_total = low_total + eb_in[5].astype(F32) + eb_in[6].astype(F32)
    fgrad_ref[:, HALF:] = low_total.T.astype(BF16)
    for d in range(1, NQ):
        arrive(("w6", d), w_all.at[(rep + NQ - d) % NQ], rep_peer(NQ - d))
    for q in range(NQ):
        done = w_all[q].astype(F32)
        for n in range(NZ):
            up, side = 32 * q + 8 * (n // 2), HALF * (n % 2)
            wgrad_ref[up : up + 8, side : side + HALF] = done[8 * n : 8 * n + 8]
    arrive("ey", ey_in, far_y)
    fgrad_ref[:, :HALF] = (run[0, rows_of[0]] + ey_in[...].astype(F32)).T.astype(BF16)
    drain(0)


def local(features, tiles, tile_target, tile_count, weight, cotangent):
    vmem = pl.BlockSpec(memory_space=pltpu.VMEM)
    hbm = pl.BlockSpec(memory_space=pltpu.HBM)

    def buf(*shape, dtype=BF16):
        return pltpu.VMEM(shape, dtype)

    return pl.pallas_call(
        kernel,
        out_shape=(
            jax.ShapeDtypeStruct((T, T), BF16),
            jax.ShapeDtypeStruct((T, T), BF16),
            jax.ShapeDtypeStruct((T, T), F32),
        ),
        in_specs=[hbm] * 6,
        out_specs=(vmem, vmem, vmem),
        scratch_shapes=[
            pltpu.SMEM((1, SLOTS), jnp.int32),
            pltpu.SMEM((1, NC), jnp.int32),
            buf(T, T),
            buf(T, T),
            buf(2, NC, T, HALF),
            buf(SLOTS, T, T),
            buf(SLOTS + 1, T, T, dtype=F32),
            pltpu.SMEM((NQ,), jnp.int32),
            buf(NQ + 1, T, T),
            buf(6, T, HALF),
            buf(6, T, HALF),
            buf(3, T, HALF),
            buf(3, T, HALF),
            buf(4, T, HALF),
            buf(4, T, HALF),
            buf(T, HALF),
            buf(T, HALF),
            buf(T, T, dtype=F32),
            buf(16, T, T),
            buf(16, T, T),
            buf(14, HALF, T),
            buf(14, HALF, T),
            buf(7, HALF, T),
            buf(7, HALF, T),
            buf(8, HALF, T),
            buf(8, HALF, T),
            buf(HALF, T),
            buf(HALF, T),
            buf(NQ, NZ * 8, HALF),
            buf(NQ - 1, NZ * 8, HALF),
            buf(NZ, 8, HALF, dtype=F32),
            buf(3, NZ, 8, HALF, dtype=F32),
            buf(NZ, 8, HALF, dtype=F32),
            buf(NZ - 1, 8, HALF, dtype=F32),
            buf(NZ, 8, HALF, dtype=F32),
            buf(NQ, NZ * 8, HALF),
            pltpu.SemaphoreType.DMA((TILE_PARTS,)),
            pltpu.SemaphoreType.DMA((6,)),
            pltpu.SemaphoreType.DMA((SENDS,)),
            pltpu.SemaphoreType.DMA((SENDS,)),
        ],
        compiler_params=pltpu.CompilerParams(
            collective_id=0, has_side_effects=True, vmem_limit_bytes=46 * 1024 * 1024
        ),
        name="graph_layer",
    )(*[
        pltpu.with_memory_space_constraint(value, pltpu.HBM)
        for value in (features, tiles, tile_target, tile_count, weight, cotangent)
    ])


def solution(mesh):
    return jax.shard_map(
        local,
        mesh=mesh,
        in_specs=(
            P(("row", "rep"), None),
            P(("row", "rep"), None, None),
            P(("row", "rep"), None),
            P(("row", "rep"), None),
            P(),
            P(("row", "rep"), None),
        ),
        out_specs=(P(("row", "rep"), None), P(("row", "rep"), None), P()),
        check_vma=False,
    )
```
